512 devices in a mesh: context: 64 (over x, z), head: 8 (over y, core).
Axes of the slice: x: 4, y: 4, z: 16, core: 2. Of those that a mesh axis runs over, the one named last changes fastest.
Arguments:
- query: bfloat16 [32768, 2048], P(('context', 'head')), may hold values from -96 to 96
- key: bfloat16 [32768, 2048], P(('context', 'head')), may hold values from -12 to 12
- value: bfloat16 [32768, 2048], P(('context', 'head')), may hold values from -12 to 12
- cotangent: bfloat16 [32768, 2048], P(('context', 'head')), may hold values from -6 to 6
Outputs:
- attended: bfloat16 [32768, 2048], P('context', 'head')
- query_gradient: bfloat16 [32768, 2048], P('context', 'head')
- grad_key: bfloat16 [32768, 2048], P('context', 'head')
- grad_value: bfloat16 [32768, 2048], P('context', 'head')
The draws below stay inside these ranges and needn't reach their ends.
All inputs are finite; a program needn't handle non-finite values.
Results may differ from the reference program's by a relative error of at most 0.019.
Values may be sent and summed in bfloat16 or wider, within the bound.
No kernel may reach another device: no remote copies, remote signals or barrier semaphores. Data moves between devices by JAX's collectives and lax.ppermute only.
A program may use at most 64 MiB of HBM per device.

```python
import math
import jax
import jax.numpy as jnp
from jax import lax

HEADS = 16
HEAD_DIM = 128
LEAF = 256
RATIO = 16
TOK_DEV = 512
D = 2048
SEQ = 32768
SUMMARY = 32
LEVELS = 6
N_CONTEXT = 64


def regions(base):
    span_width = HEADS * HEAD_DIM
    total = jnp.zeros((SEQ, span_width), jnp.float32)
    smallest = LEAF // 2
    for region_index in range((SEQ // smallest).bit_length()):
        rows_per_span = smallest << region_index
        table = jax.random.normal(jax.random.fold_in(base, 100 + region_index), (SEQ // rows_per_span, span_width), jnp.float32)
        total = total + 0.3 * jnp.repeat(table, rows_per_span, axis=0)
    return total


def rough_field(base):
    span_width = HEADS * HEAD_DIM
    gauss = jax.random.normal(jax.random.fold_in(base, 1), (SEQ, span_width), jnp.float32)
    return gauss + regions(jax.random.fold_in(base, 4))


def widened(field, base):
    chosen = jax.random.randint(jax.random.fold_in(base, 9), (), 0, SEQ)
    position = jnp.arange(SEQ, dtype=jnp.int32)
    return jnp.where((position == chosen)[:, None], 6.0 * field, field)


def shared_keys(key):
    field = rough_field(jax.random.fold_in(key, 1))
    return jnp.clip(field, -12.0, 12.0)


def draw_key(key, part):
    field = shared_keys(key)
    field = jnp.clip(widened(field, jax.random.fold_in(key, 5)), -12.0, 12.0)
    return field.astype(jnp.bfloat16)


def draw_query(key, part):
    own = jax.random.fold_in(key, 7)
    span_width = HEADS * HEAD_DIM
    gauss = jnp.clip(jax.random.normal(jax.random.fold_in(own, 1), (SEQ, span_width), jnp.float32), -6.0, 6.0)
    queries = gauss
    return jnp.clip(queries, -96.0, 96.0).astype(jnp.bfloat16)


def draw_value(key, part):
    own = jax.random.fold_in(key, 3)
    field = rough_field(own)
    field = widened(field, own)
    return jnp.clip(field, -12.0, 12.0).astype(jnp.bfloat16)


def level_of(stream_key, shape, cuts, low, largest):
    factor_of, own = 1.0, jax.random.fold_in(stream_key, 6)
    for dim, blocks in cuts:
        heights = jnp.exp(jax.random.uniform(jax.random.fold_in(own, dim), (blocks,), jnp.float32, low / len(cuts), largest / len(cuts)))
        factor_of = factor_of * jnp.repeat(heights, shape[dim] // blocks).reshape([-1 if axis == dim else 1 for axis in range(len(shape))])
    return factor_of


def scatter_about(own_key, shape, scale, most, split=(), kind=jnp.bfloat16):
    values = scale * jax.random.normal(own_key, shape, jnp.float32)
    if split:
        values = values * level_of(own_key, shape, split, -0.22, 0.18)
    return jnp.clip(values, -most, most).astype(kind)


def setup_inputs(seed: int = 0) -> dict:
    splits = jax.random.split(jax.random.key(seed), 5)
    query = draw_query(jax.random.fold_in(splits[4], 71), 0)
    key = draw_key(jax.random.fold_in(splits[4], 71), 0)
    value = draw_value(jax.random.fold_in(splits[4], 71), 0)
    cotangent = scatter_about(splits[3], (SEQ, D), 1.0, 6.0, ((0, 512),))
    return {"query": query, "key": key, "value": value, "cotangent": cotangent}


def product(form, left, right):
    return jnp.einsum(form, left.astype(jnp.float32), right.astype(jnp.float32))


def windows(framed):
    return jnp.concatenate([framed[:-2], framed[1:-1], framed[2:]], axis=1)


def unfold(window_grad):
    blocks = window_grad.shape[0]
    parts = window_grad.reshape(blocks, 3, LEAF, -1)
    spread = jnp.pad(parts[:, 0], ((0, 2), (0, 0), (0, 0)))
    spread = spread + jnp.pad(parts[:, 1], ((1, 1), (0, 0), (0, 0)))
    spread = spread + jnp.pad(parts[:, 2], ((2, 0), (0, 0), (0, 0)))
    return spread.reshape((blocks + 2) * LEAF, -1)


def attend(queries, key_ext, value_ext, grad_out, coarse_keys, coarse_values, valid):
    tokens, span_width = queries.shape
    heads = span_width // HEAD_DIM
    blocks = tokens // LEAF
    factor = HEAD_DIM ** -0.5
    query_four = queries.reshape(blocks, LEAF, heads, HEAD_DIM)
    grad_four = grad_out.reshape(blocks, LEAF, heads, HEAD_DIM)
    key_win = windows(key_ext.reshape(blocks + 2, LEAF, heads, HEAD_DIM))
    value_win = windows(value_ext.reshape(blocks + 2, LEAF, heads, HEAD_DIM))
    allowed = windows(valid.reshape(blocks + 2, LEAF))
    coarse_k = coarse_keys.reshape(-1, heads, HEAD_DIM)
    coarse_v = coarse_values.reshape(-1, heads, HEAD_DIM)
    near = product("bqhd,bkhd->bhqk", query_four, key_win) * factor
    near = jnp.where(allowed[:, None, None, :], near, -1e30)
    far = product("bqhd,khd->bhqk", query_four, coarse_k) * factor + math.log(RATIO)
    top = jnp.maximum(jnp.max(near, axis=-1), jnp.max(far, axis=-1))
    near_exp = jnp.exp(near - top[..., None])
    far_exp = jnp.exp(far - top[..., None])
    total = jnp.sum(near_exp, axis=-1) + jnp.sum(far_exp, axis=-1)
    near_prob = near_exp / total[..., None]
    far_prob = far_exp / total[..., None]
    near_low = near_prob.astype(jnp.bfloat16)
    far_low = far_prob.astype(jnp.bfloat16)
    mixed_output = product("bhqk,bkhd->bqhd", near_low, value_win) + product("bhqk,khd->bqhd", far_low, coarse_v)
    delta = jnp.transpose(jnp.sum(grad_four.astype(jnp.float32) * mixed_output, axis=-1), (0, 2, 1))
    near_dprob = product("bqhd,bkhd->bhqk", grad_four, value_win)
    far_dprob = product("bqhd,khd->bhqk", grad_four, coarse_v)
    near_dscore = (near_prob * (near_dprob - delta[..., None])).astype(jnp.bfloat16)
    far_dscore = (far_prob * (far_dprob - delta[..., None])).astype(jnp.bfloat16)
    query_gradient = (product("bhqk,bkhd->bqhd", near_dscore, key_win) + product("bhqk,khd->bqhd", far_dscore, coarse_k)) * factor
    key_grad_win = product("bhqk,bqhd->bkhd", near_dscore, query_four) * factor
    value_grad_win = product("bhqk,bqhd->bkhd", near_low, grad_four)
    coarse_kgrad = product("bhqk,bqhd->khd", far_dscore, query_four) * factor
    coarse_vgrad = product("bhqk,bqhd->khd", far_low, grad_four)
    return (mixed_output.astype(jnp.bfloat16).reshape(tokens, span_width), query_gradient.reshape(tokens, span_width),
            unfold(key_grad_win), unfold(value_grad_win),
            coarse_kgrad.reshape(-1, span_width), coarse_vgrad.reshape(-1, span_width), (top, total, delta))


def pooled(source, rows_per_span):
    sequence_length, span_width = source.shape
    return jnp.sum(source.reshape(sequence_length // rows_per_span, rows_per_span, span_width), axis=1, dtype=jnp.float32) / rows_per_span


def reference(query, key, value, cotangent):
    sequence_length, span_width = query.shape
    group_summary = SUMMARY
    pooled_keys = [pooled(key, RATIO << tree_level_index) for tree_level_index in range(LEVELS)]
    pooled_values = [pooled(value, RATIO << tree_level_index) for tree_level_index in range(LEVELS)]
    key_padded = jnp.pad(key, ((LEAF, LEAF), (0, 0)))
    value_padded = jnp.pad(value, ((LEAF, LEAF), (0, 0)))

    def one_range(loop_carry, range_index):
        key_accumulator, value_accumulator, pooled_key_accumulator, pooled_value_accumulator = loop_carry
        start = range_index * TOK_DEV
        queries = lax.dynamic_slice_in_dim(query, start, TOK_DEV, 0)
        grad_out = lax.dynamic_slice_in_dim(cotangent, start, TOK_DEV, 0)
        key_ext = lax.dynamic_slice_in_dim(key_padded, start, TOK_DEV + 2 * LEAF, 0)
        value_ext = lax.dynamic_slice_in_dim(value_padded, start, TOK_DEV + 2 * LEAF, 0)
        position = start - LEAF + jnp.arange(TOK_DEV + 2 * LEAF, dtype=jnp.int32)
        valid = (position >= 0) & (position < sequence_length)
        sibling_rows = []
        for tree_level_index in range(LEVELS):
            group = range_index // (1 << tree_level_index)
            sibling_rows.append(((group + 1 - 2 * (group % 2)) * group_summary).astype(jnp.int32))
        coarse_keys = jnp.concatenate([lax.dynamic_slice_in_dim(pooled_keys[tree_level_index], sibling_rows[tree_level_index], group_summary, 0) for tree_level_index in range(LEVELS)], axis=0).astype(jnp.bfloat16)
        coarse_values = jnp.concatenate([lax.dynamic_slice_in_dim(pooled_values[tree_level_index], sibling_rows[tree_level_index], group_summary, 0) for tree_level_index in range(LEVELS)], axis=0).astype(jnp.bfloat16)
        result = attend(queries, key_ext, value_ext, grad_out, coarse_keys, coarse_values, valid)
        mixed_output, query_gradient, key_ext_grad, value_ext_grad, coarse_kgrad, coarse_vgrad, unused = result
        key_accumulator = lax.dynamic_update_slice_in_dim(key_accumulator, lax.dynamic_slice_in_dim(key_accumulator, start, TOK_DEV + 2 * LEAF, 0) + key_ext_grad, start, 0)
        value_accumulator = lax.dynamic_update_slice_in_dim(value_accumulator, lax.dynamic_slice_in_dim(value_accumulator, start, TOK_DEV + 2 * LEAF, 0) + value_ext_grad, start, 0)
        updated_key_accumulator = []
        updated_value_accumulator = []
        for tree_level_index in range(LEVELS):
            row_count = sibling_rows[tree_level_index]
            piece_k = coarse_kgrad[tree_level_index * group_summary:(tree_level_index + 1) * group_summary]
            value_piece = coarse_vgrad[tree_level_index * group_summary:(tree_level_index + 1) * group_summary]
            updated_key_accumulator.append(lax.dynamic_update_slice_in_dim(pooled_key_accumulator[tree_level_index], lax.dynamic_slice_in_dim(pooled_key_accumulator[tree_level_index], row_count, group_summary, 0) + piece_k, row_count, 0))
            updated_value_accumulator.append(lax.dynamic_update_slice_in_dim(pooled_value_accumulator[tree_level_index], lax.dynamic_slice_in_dim(pooled_value_accumulator[tree_level_index], row_count, group_summary, 0) + value_piece, row_count, 0))
        return (key_accumulator, value_accumulator, tuple(updated_key_accumulator), tuple(updated_value_accumulator)), (mixed_output, query_gradient.astype(jnp.bfloat16))

    start_carry = (jnp.zeros((sequence_length + 2 * LEAF, span_width), jnp.float32),
                   jnp.zeros((sequence_length + 2 * LEAF, span_width), jnp.float32),
                   tuple(jnp.zeros(pooled_keys[tree_level_index].shape, jnp.float32) for tree_level_index in range(LEVELS)),
                   tuple(jnp.zeros(pooled_keys[tree_level_index].shape, jnp.float32) for tree_level_index in range(LEVELS)))
    final_result, outputs = lax.scan(one_range, start_carry, jnp.arange(N_CONTEXT, dtype=jnp.int32))
    key_accumulator, value_accumulator, pooled_key_accumulator, pooled_value_accumulator = final_result
    key_total = key_accumulator[LEAF:LEAF + sequence_length]
    total_value_sum = value_accumulator[LEAF:LEAF + sequence_length]
    for tree_level_index in range(LEVELS):
        rows_per_span = RATIO << tree_level_index
        key_total = (key_total.reshape(sequence_length // rows_per_span, rows_per_span, span_width) + (pooled_key_accumulator[tree_level_index] / rows_per_span)[:, None, :]).reshape(sequence_length, span_width)
        total_value_sum = (total_value_sum.reshape(sequence_length // rows_per_span, rows_per_span, span_width) + (pooled_value_accumulator[tree_level_index] / rows_per_span)[:, None, :]).reshape(sequence_length, span_width)
    attended = outputs[0].reshape(sequence_length, span_width)
    query_gradient = outputs[1].reshape(sequence_length, span_width)
    return attended, query_gradient, key_total.astype(jnp.bfloat16), total_value_sum.astype(jnp.bfloat16)
```

```python
import math

import jax
import jax.numpy as jnp
from jax import lax
from jax.experimental import pallas as pl
from jax.experimental.pallas import tpu as pltpu
from jax.sharding import PartitionSpec as P

HEAD_DIM = 128
LEAF = 256
RATIO = 16
TOKENS = 512
SPAN = 256
SHARES = 8
SHARE = 64
LEVELS = 6
OWN = 64
COUNT = [32 >> level for level in range(LEVELS)]
START = [64 - (64 >> level) for level in range(LEVELS)]
MESSAGE = [(16 >> b) * (7 - b) if b < 5 else 1 for b in range(LEVELS)]
HELD = [sum(MESSAGE[b + 1 :]) for b in range(LEVELS)]
COARSE = sum(MESSAGE)
F32 = jnp.float32
BF16 = jnp.bfloat16
VMEM = pl.BlockSpec(memory_space=pltpu.VMEM)
SMEM = pl.BlockSpec(memory_space=pltpu.SMEM)
LIMIT = pltpu.CompilerParams(vmem_limit_bytes=48 * 1024 * 1024)


def dot(left, right, over):
    return lax.dot_general(left, right, (over, ((), ())), preferred_element_type=F32)


NN = ((1,), (0,))
NT = ((1,), (1,))


def call(kernel, out_shape, scratch=(), specs=None, count=1):
    return pl.pallas_call(
        kernel,
        out_shape=out_shape,
        in_specs=specs or [VMEM] * count,
        out_specs=jax.tree.map(lambda _: VMEM, out_shape),
        scratch_shapes=scratch,
        compiler_params=LIMIT,
    )


def shape(rows, columns, kind=BF16):
    return jax.ShapeDtypeStruct((rows, columns), kind)


def pack_kernel(first, second, packed):
    for share in range(SHARES):
        columns = slice(share * SPAN, (share + 1) * SPAN)
        packed[share, :SHARE, :] = first[:, columns]
        packed[share, SHARE:, :] = second[:, columns]


def pack(first, second):
    out = jax.ShapeDtypeStruct((SHARES, 2 * SHARE, SPAN), BF16)
    return call(pack_kernel, out, count=2)(first, second)


def member(rows, columns, row_axis):
    row = lax.broadcasted_iota(jnp.int32, (rows, columns), row_axis)
    token = lax.broadcasted_iota(jnp.int32, (rows, columns), 1 - row_axis)
    weight = jnp.zeros((rows, columns), F32)
    for level in range(LEVELS):
        shift = 4 + level
        hit = row == START[level] + lax.shift_right_logical(token, shift)
        weight = jnp.where(hit, 1.0 / (1 << shift), weight)
    return weight.astype(BF16)


def pool_kernel(kv, pooled):
    weight = member(OWN, TOKENS, 0)
    for part in range(2):
        rows = kv[:, part * SHARE : (part + 1) * SHARE, :].reshape(TOKENS, SPAN)
        pooled[:, part * SPAN : (part + 1) * SPAN] = dot(weight, rows, NN).astype(BF16)


def attend_kernel(
    spot, kv, low, high, qg, coarse,
    attended, query_grad, centre, to_prev, to_next, coarse_grad,
    keys, values, key_grad, value_grad,
):
    factor = HEAD_DIM ** (-0.5)
    binary = factor * math.log2(math.e)
    position = spot[0]
    bias_low = jnp.where(position == 0, -1e30, 0.0).astype(F32)
    bias_high = jnp.where(position == spot[1] - 1, -1e30, 0.0).astype(F32)
    for head in range(2):
        columns = slice(head * HEAD_DIM, (head + 1) * HEAD_DIM)
        for part, store in ((0, keys), (1, values)):
            rows = slice(part * SHARE, (part + 1) * SHARE)
            store[:LEAF, :] = low[:, rows, columns].reshape(LEAF, HEAD_DIM)
            store[LEAF : LEAF + TOKENS, :] = kv[:, rows, columns].reshape(TOKENS, HEAD_DIM)
            store[LEAF + TOKENS :, :] = high[:, rows, columns].reshape(LEAF, HEAD_DIM)
        far_key = coarse[:, head * HEAD_DIM : (head + 1) * HEAD_DIM]
        far_value = coarse[:, SPAN + head * HEAD_DIM : SPAN + (head + 1) * HEAD_DIM]
        key_t = jnp.transpose(keys[...])
        value_t = jnp.transpose(values[...])
        far_key_t = jnp.transpose(far_key)
        far_value_t = jnp.transpose(far_value)
        far_key_grad = jnp.zeros((COARSE, HEAD_DIM), F32)
        far_value_grad = jnp.zeros((COARSE, HEAD_DIM), F32)
        for block in range(2):
            query = qg[4 * block : 4 * block + 4, :SHARE, columns].reshape(LEAF, HEAD_DIM)
            grad = qg[4 * block : 4 * block + 4, SHARE:, columns].reshape(LEAF, HEAD_DIM)
            window = slice(block * LEAF, block * LEAF + 3 * LEAF)
            near = dot(keys[window, :], query, NT) * binary
            if block == 0:
                near = jnp.concatenate([near[:LEAF] + bias_low, near[LEAF:]], axis=0)
            else:
                near = jnp.concatenate([near[: 2 * LEAF], near[2 * LEAF :] + bias_high], axis=0)
            far = dot(far_key, query, NT) * binary + math.log2(RATIO)
            top = jnp.maximum(
                jnp.max(near, axis=0, keepdims=True), jnp.max(far, axis=0, keepdims=True)
            )
            near = jnp.exp2(near - top)
            far = jnp.exp2(far - top)
            total = jnp.sum(near, axis=0, keepdims=True) + jnp.sum(far, axis=0, keepdims=True)
            inverse = 1.0 / total
            near = near * inverse
            far = far * inverse
            near_low = near.astype(BF16)
            far_low = far.astype(BF16)
            mixed_t = dot(value_t[:, window], near_low, NN) + dot(far_value_t, far_low, NN)
            grad_t = jnp.transpose(grad.astype(F32))
            delta = jnp.sum(grad_t * mixed_t, axis=0, keepdims=True)
            near_score = (near * (dot(values[window, :], grad, NT) - delta)).astype(BF16)
            far_score = (far * (dot(far_value, grad, NT) - delta)).astype(BF16)
            query_t = dot(key_t[:, window], near_score, NN) + dot(far_key_t, far_score, NN)
            out = slice(block * LEAF, (block + 1) * LEAF)
            attended[out, columns] = jnp.transpose(mixed_t).astype(BF16)
            query_grad[out, columns] = jnp.transpose(query_t * factor).astype(BF16)
            near_key_grad = dot(near_score, query, NN) * factor
            near_value_grad = dot(near_low, grad, NN)
            far_key_grad = far_key_grad + dot(far_score, query, NN) * factor
            far_value_grad = far_value_grad + dot(far_low, grad, NN)
            if block == 0:
                key_grad[: 3 * LEAF, :] = near_key_grad
                value_grad[: 3 * LEAF, :] = near_value_grad
            else:
                key_grad[LEAF : 3 * LEAF, :] += near_key_grad[: 2 * LEAF]
                value_grad[LEAF : 3 * LEAF, :] += near_value_grad[: 2 * LEAF]
                key_grad[3 * LEAF :, :] = near_key_grad[2 * LEAF :]
                value_grad[3 * LEAF :, :] = near_value_grad[2 * LEAF :]
        for part, store, far_grad in ((0, key_grad, far_key_grad), (1, value_grad, far_value_grad)):
            place = slice(part * SPAN + head * HEAD_DIM, part * SPAN + (head + 1) * HEAD_DIM)
            to_prev[:, place] = store[:LEAF, :].astype(BF16)
            centre[:, place] = store[LEAF : LEAF + TOKENS, :]
            to_next[:, place] = store[LEAF + TOKENS :, :].astype(BF16)
            coarse_grad[:, place] = far_grad


def finish_kernel(centre, from_prev, from_next, pooled, key_grad, value_grad):
    weight = member(TOKENS, OWN, 1)
    spread = dot(weight, pooled[...], NN) + centre[...]
    low = spread[:LEAF] + from_prev[...].astype(F32)
    high = spread[LEAF:] + from_next[...].astype(F32)
    key_grad[:LEAF, :] = low[:, :SPAN].astype(BF16)
    key_grad[LEAF:, :] = high[:, :SPAN].astype(BF16)
    value_grad[:LEAF, :] = low[:, SPAN:].astype(BF16)
    value_grad[LEAF:, :] = high[:, SPAN:].astype(BF16)


def body(query, key, value, cotangent):
    devices = lax.axis_size("context")
    position = lax.axis_index("context")

    def ring(block, step):
        pairs = [(source, (source + step) % devices) for source in range(devices)]
        return lax.ppermute(block, "context", pairs)

    def partner(block, bit):
        pairs = [(source, source ^ (1 << bit)) for source in range(devices)]
        return lax.ppermute(block, "context", pairs)

    kv = lax.all_to_all(pack(key, value), "head", 0, 0)
    qg = lax.all_to_all(pack(query, cotangent), "head", 0, 0)
    low = ring(kv[4:], 1)
    high = ring(kv[:4], -1)
    pooled = call(pool_kernel, shape(OWN, 2 * SPAN))(kv)
    held = jnp.zeros((0, 2 * SPAN), BF16)
    for bit in reversed(range(LEVELS)):
        own = pooled[START[bit] : START[bit] + COUNT[bit]]
        held = jnp.concatenate([held, partner(jnp.concatenate([own, held]), bit)])
    attended, query_grad, centre, to_prev, to_next, coarse_grad = call(
        attend_kernel,
        (
            shape(TOKENS, SPAN),
            shape(TOKENS, SPAN),
            shape(TOKENS, 2 * SPAN, F32),
            shape(LEAF, 2 * SPAN),
            shape(LEAF, 2 * SPAN),
            shape(COARSE, 2 * SPAN, F32),
        ),
        [
            pltpu.VMEM((2 * LEAF + TOKENS, HEAD_DIM), BF16),
            pltpu.VMEM((2 * LEAF + TOKENS, HEAD_DIM), BF16),
            pltpu.VMEM((2 * LEAF + TOKENS, HEAD_DIM), F32),
            pltpu.VMEM((2 * LEAF + TOKENS, HEAD_DIM), F32),
        ],
        [SMEM] + [VMEM] * 5,
    )(jnp.stack([position, jnp.int32(devices)]), kv, low, high, qg, held)
    from_next = ring(to_prev, -1)
    from_prev = ring(to_next, 1)
    rest = coarse_grad
    own_grads = []
    for bit in range(LEVELS):
        back = partner(rest[HELD[bit] :].astype(BF16), bit)
        own_grads.append(back[: COUNT[bit]])
        rest = rest[: HELD[bit]] + back[COUNT[bit] :].astype(F32)
    own_grads.append(jnp.zeros((1, 2 * SPAN), BF16))
    key_grad, value_grad = call(
        finish_kernel, (shape(TOKENS, SPAN), shape(TOKENS, SPAN)), count=4
    )(centre, from_prev, from_next, jnp.concatenate(own_grads))
    return attended, query_grad, key_grad, value_grad


def solution(mesh):
    spec = P(("context", "head"), None)
    out = P("context", "head")
    return jax.shard_map(
        body, mesh=mesh, in_specs=(spec,) * 4, out_specs=(out,) * 4, check_vma=False
    )
```

```python
import math

import jax
import jax.numpy as jnp
from jax import lax
from jax.experimental import pallas as pl
from jax.experimental.pallas import tpu as pltpu
from jax.sharding import PartitionSpec as P

HEAD_DIM = 128
LEAF = 256
RATIO = 16
TOKENS = 512
SPAN = 256
SHARES = 8
SHARE = 64
LEVELS = 6
OWN = 64
COUNT = [32 >> level for level in range(LEVELS)]
START = [64 - (64 >> level) for level in range(LEVELS)]
PEERS = 8
FAR_ROWS = 8
NEAR_ROWS = 32
HELD = 12
NEAR = PEERS * NEAR_ROWS
COARSE = NEAR + COUNT[0]
F32 = jnp.float32
BF16 = jnp.bfloat16
VMEM = pl.BlockSpec(memory_space=pltpu.VMEM)
SMEM = pl.BlockSpec(memory_space=pltpu.SMEM)
LIMIT = pltpu.CompilerParams(vmem_limit_bytes=48 * 1024 * 1024)
NN = ((1,), (0,))
NT = ((1,), (1,))


def dot(left, right, over):
    return lax.dot_general(left, right, (over, ((), ())), preferred_element_type=F32)


def call(kernel, out_shape, scratch=(), specs=None, count=1):
    return pl.pallas_call(
        kernel,
        out_shape=out_shape,
        in_specs=specs or [VMEM] * count,
        out_specs=jax.tree.map(lambda _: VMEM, out_shape),
        scratch_shapes=scratch,
        compiler_params=LIMIT,
    )


def shape(*sizes, kind=BF16):
    return jax.ShapeDtypeStruct(sizes, kind)


def grid(rows, columns):
    return (
        lax.broadcasted_iota(jnp.int32, (rows, columns), 0),
        lax.broadcasted_iota(jnp.int32, (rows, columns), 1),
    )


def ones(hit):
    return jnp.where(hit, 1.0, 0.0).astype(BF16)


def pick(index, cases, last):
    result = last
    for bound, value in reversed(cases):
        result = jnp.where(index < bound, value, result)
    return result


def far_slot(offset, row):
    count = pick(offset, [(1, 0), (2, 4), (4, 2)], 1)
    start = pick(offset, [(2, START[3]), (4, START[4])], START[5])
    return row < count, start + row


def near_slot(offset, row):
    own = row - HELD
    count = pick(offset, [(2, 0), (4, COUNT[1])], COUNT[2])
    start = pick(offset, [(4, START[1])], START[2])
    return (own >= 0) & (own < count), start + own


def held_slot(row):
    offset = pick(row, [(4, 1), (6, 2), (8, 3)], row - 4)
    return row < HELD, offset, pick(row, [(4, row), (8, row & 1)], 0)


def pack_kernel(key, value, query, cotangent, packed):
    for share in range(SHARES):
        columns = slice(share * SPAN, (share + 1) * SPAN)
        for part, source in enumerate((key, value, query, cotangent)):
            packed[share, part * SHARE : (part + 1) * SHARE, :] = source[:, columns]


def pack(*sources):
    return call(pack_kernel, shape(SHARES, 4 * SHARE, SPAN), count=4)(*sources)


def pool_kernel(spot, whole, pooled, far_send, to_next, to_prev):
    row, token = grid(OWN, TOKENS)
    weight = jnp.zeros((OWN, TOKENS), F32)
    for level in range(LEVELS):
        shift = 4 + level
        hit = row == START[level] + lax.shift_right_logical(token, shift)
        weight = jnp.where(hit, 1.0 / (1 << shift), weight)
    weight = weight.astype(BF16)
    for part in range(2):
        rows = whole[:, part * SHARE : (part + 1) * SHARE, :].reshape(TOKENS, SPAN)
        means = dot(weight, rows, NN).astype(BF16)
        pooled[:, part * SPAN : (part + 1) * SPAN] = means
        place = slice(TOKENS + part * COUNT[0], TOKENS + (part + 1) * COUNT[0])
        to_next[place, :] = means[: COUNT[0]]
        to_prev[place, :] = means[: COUNT[0]]
    row, column = grid(OWN, OWN)
    valid, source = far_slot((row >> 3) ^ (spot[0] >> 3), row & 7)
    far_send[...] = (
        dot(ones(valid & (column == source)), pooled[...], NN)
        .astype(BF16)
        .reshape(PEERS, FAR_ROWS, 2 * SPAN)
    )
    to_prev[:TOKENS, :] = whole[: SHARES // 2, : 2 * SHARE, :].reshape(TOKENS, SPAN)
    to_next[:TOKENS, :] = whole[SHARES // 2 :, : 2 * SHARE, :].reshape(TOKENS, SPAN)


def near_kernel(spot, pooled, far, near_send):
    far_at, near_at = spot[0] >> 3, spot[0] & 7
    row, column = grid(NEAR, OWN)
    inside = row & (NEAR_ROWS - 1)
    valid, source = near_slot((row >> 5) ^ near_at, inside)
    own = dot(ones(valid & (column == source)), pooled[...], NN)
    valid, offset, place = held_slot(inside)
    hit = valid & (column == (offset ^ far_at) * FAR_ROWS + place)
    held = dot(ones(hit), far[...].reshape(PEERS * FAR_ROWS, 2 * SPAN), NN)
    near_send[...] = (own + held).astype(BF16).reshape(PEERS, NEAR_ROWS, 2 * SPAN)


def far_kernel(spot, near, far_send):
    row, column = grid(OWN, NEAR)
    valid, offset, place = held_slot(column & (NEAR_ROWS - 1))
    hit = valid & (offset == ((row >> 3) ^ (spot[0] >> 3))) & (place == (row & 7))
    far_send[...] = (
        dot(ones(hit), near[...].reshape(NEAR, 2 * SPAN), NN)
        .astype(BF16)
        .reshape(PEERS, FAR_ROWS, 2 * SPAN)
    )


def attend_kernel(
    spot, whole, low, high, near_rows,
    attended, query_grad, centre, to_prev, to_next, near_send,
    keys, values, key_grad, value_grad, far_keys, far_values,
):
    factor = HEAD_DIM ** (-0.5)
    binary = factor * math.log2(math.e)
    position = spot[0]
    bias_low = jnp.where(position == 0, -1e30, 0.0).astype(F32)
    bias_high = jnp.where(position == spot[1] - 1, -1e30, 0.0).astype(F32)
    even = (position & 1) == 0
    row = lax.broadcasted_iota(jnp.int32, (COARSE, LEAF), 0)
    inside = row & (NEAR_ROWS - 1)
    valid, _ = near_slot((row >> 5) ^ (position & 7), inside)
    valid = valid | (inside < HELD) | (row >= NEAR)
    far_bias = jnp.where(valid, math.log2(RATIO), -1e30)
    for head in range(2):
        columns = slice(head * HEAD_DIM, (head + 1) * HEAD_DIM)
        for part, store, far_store in ((0, keys, far_keys), (1, values, far_values)):
            rows = slice(part * SHARE, (part + 1) * SHARE)
            place = slice(part * SPAN + head * HEAD_DIM, part * SPAN + (head + 1) * HEAD_DIM)
            level_zero = slice(TOKENS + part * COUNT[0], TOKENS + (part + 1) * COUNT[0])
            half = SHARES // 2
            store[:LEAF, :] = (
                low[:TOKENS, columns].reshape(half, 2 * SHARE, HEAD_DIM)[:, rows].reshape(LEAF, HEAD_DIM)
            )
            store[LEAF : LEAF + TOKENS, :] = whole[:, rows, columns].reshape(TOKENS, HEAD_DIM)
            store[LEAF + TOKENS :, :] = (
                high[:TOKENS, columns].reshape(half, 2 * SHARE, HEAD_DIM)[:, rows].reshape(LEAF, HEAD_DIM)
            )
            far_store[:NEAR, :] = near_rows[:, :, place].reshape(NEAR, HEAD_DIM)

            @pl.when(even)
            def _():
                far_store[NEAR:, :] = high[level_zero, columns]

            @pl.when(jnp.logical_not(even))
            def _():
                far_store[NEAR:, :] = low[level_zero, columns]

        far_key = far_keys[...]
        far_value = far_values[...]
        key_t = jnp.transpose(keys[...])
        value_t = jnp.transpose(values[...])
        far_key_t = jnp.transpose(far_key)
        far_value_t = jnp.transpose(far_value)
        far_key_grad = jnp.zeros((COARSE, HEAD_DIM), F32)
        far_value_grad = jnp.zeros((COARSE, HEAD_DIM), F32)
        for block in range(2):
            query = whole[4 * block : 4 * block + 4, 2 * SHARE : 3 * SHARE, columns].reshape(LEAF, HEAD_DIM)
            grad = whole[4 * block : 4 * block + 4, 3 * SHARE :, columns].reshape(LEAF, HEAD_DIM)
            window = slice(block * LEAF, block * LEAF + 3 * LEAF)
            near = dot(keys[window, :], query, NT) * binary
            if block == 0:
                near = jnp.concatenate([near[:LEAF] + bias_low, near[LEAF:]], axis=0)
            else:
                near = jnp.concatenate([near[: 2 * LEAF], near[2 * LEAF :] + bias_high], axis=0)
            far = dot(far_key, query, NT) * binary + far_bias
            top = jnp.maximum(
                jnp.max(near, axis=0, keepdims=True), jnp.max(far, axis=0, keepdims=True)
            )
            near = jnp.exp2(near - top)
            far = jnp.exp2(far - top)
            total = jnp.sum(near, axis=0, keepdims=True) + jnp.sum(far, axis=0, keepdims=True)
            inverse = 1.0 / total
            near = near * inverse
            far = far * inverse
            near_low = near.astype(BF16)
            far_low = far.astype(BF16)
            mixed_t = dot(value_t[:, window], near_low, NN) + dot(far_value_t, far_low, NN)
            grad_t = jnp.transpose(grad.astype(F32))
            delta = jnp.sum(grad_t * mixed_t, axis=0, keepdims=True)
            near_score = (near * (dot(values[window, :], grad, NT) - delta)).astype(BF16)
            far_score = (far * (dot(far_value, grad, NT) - delta)).astype(BF16)
            query_t = dot(key_t[:, window], near_score, NN) + dot(far_key_t, far_score, NN)
            out = slice(block * LEAF, (block + 1) * LEAF)
            attended[out, columns] = jnp.transpose(mixed_t).astype(BF16)
            query_grad[out, columns] = jnp.transpose(query_t * factor).astype(BF16)
            near_key_grad = dot(near_score, query, NN) * factor
            near_value_grad = dot(near_low, grad, NN)
            far_key_grad = far_key_grad + dot(far_score, query, NN) * factor
            far_value_grad = far_value_grad + dot(far_low, grad, NN)
            if block == 0:
                key_grad[: 3 * LEAF, :] = near_key_grad
                value_grad[: 3 * LEAF, :] = near_value_grad
            else:
                key_grad[LEAF : 3 * LEAF, :] += near_key_grad[: 2 * LEAF]
                value_grad[LEAF : 3 * LEAF, :] += near_value_grad[: 2 * LEAF]
                key_grad[3 * LEAF :, :] = near_key_grad[2 * LEAF :]
                value_grad[3 * LEAF :, :] = near_value_grad[2 * LEAF :]
        for part, store, far_grad in ((0, key_grad, far_key_grad), (1, value_grad, far_value_grad)):
            place = slice(part * SPAN + head * HEAD_DIM, part * SPAN + (head + 1) * HEAD_DIM)
            to_prev[:LEAF, place] = store[:LEAF, :].astype(BF16)
            centre[:, place] = store[LEAF : LEAF + TOKENS, :]
            to_next[:LEAF, place] = store[LEAF + TOKENS :, :].astype(BF16)
            far_low = far_grad.astype(BF16)
            to_prev[LEAF:, place] = far_low[NEAR:]
            to_next[LEAF:, place] = far_low[NEAR:]
            near_send[:, :, place] = far_low[:NEAR].reshape(PEERS, NEAR_ROWS, HEAD_DIM)


def finish_kernel(spot, centre, from_prev, from_next, near, far, key_grad, value_grad, level_zero):
    position = spot[0]

    @pl.when((position & 1) == 0)
    def _():
        level_zero[...] = from_next[LEAF:, :]

    @pl.when((position & 1) == 1)
    def _():
        level_zero[...] = from_prev[LEAF:, :]

    token, column = grid(TOKENS, COUNT[0])
    weight = jnp.where((token >> 4) == column, 1.0 / RATIO, 0.0).astype(BF16)
    spread = centre[...] + dot(weight, level_zero[...], NN)
    token, column = grid(TOKENS, NEAR)
    offset = (column >> 5) ^ (position & 7)
    own = (column & (NEAR_ROWS - 1)) - HELD
    hit_one = (offset >= 2) & (offset < 4) & ((token >> 5) == own)
    hit_two = (offset >= 4) & ((token >> 6) == own)
    weight = jnp.where(hit_one, 1.0 / 32, jnp.where(hit_two, 1.0 / 64, 0.0)).astype(BF16)
    spread = spread + dot(weight, near[...].reshape(NEAR, 2 * SPAN), NN)
    token, column = grid(TOKENS, OWN)
    offset = (column >> 3) ^ (position >> 3)
    place = column & 7
    hit_three = (offset == 1) & ((token >> 7) == place)
    hit_four = (offset >= 2) & (offset < 4) & ((token >> 8) == place)
    hit_five = (offset >= 4) & (place == 0)
    weight = jnp.where(hit_three, 1.0 / 128, jnp.where(hit_four, 1.0 / 256, 0.0))
    weight = jnp.where(hit_five, 1.0 / 512, weight).astype(BF16)
    spread = spread + dot(weight, far[...].reshape(OWN, 2 * SPAN), NN)
    low = spread[:LEAF] + from_prev[:LEAF, :].astype(F32)
    high = spread[LEAF:] + from_next[:LEAF, :].astype(F32)
    key_grad[:LEAF, :] = low[:, :SPAN].astype(BF16)
    key_grad[LEAF:, :] = high[:, :SPAN].astype(BF16)
    value_grad[:LEAF, :] = low[:, SPAN:].astype(BF16)
    value_grad[LEAF:, :] = high[:, SPAN:].astype(BF16)


FAR_GROUPS = [[far * PEERS + near for far in range(PEERS)] for near in range(PEERS)]
NEAR_GROUPS = [[far * PEERS + near for near in range(PEERS)] for far in range(PEERS)]


def body(query, key, value, cotangent):
    devices = lax.axis_size("context")
    position = lax.axis_index("context")
    spot = jnp.stack([position, jnp.int32(devices)])

    def ring(block, step):
        pairs = [(source, (source + step) % devices) for source in range(devices)]
        return lax.ppermute(block, "context", pairs)

    def exchange(block, groups):
        return lax.all_to_all(block, "context", 0, 0, axis_index_groups=groups)

    whole = lax.all_to_all(pack(key, value, query, cotangent), "head", 0, 0)
    slots = shape(PEERS, NEAR_ROWS, 2 * SPAN)
    far_slots = shape(PEERS, FAR_ROWS, 2 * SPAN)
    rim = shape(TOKENS + 2 * COUNT[0], SPAN)
    pooled, far_send, to_next, to_prev = call(
        pool_kernel, (shape(OWN, 2 * SPAN), far_slots, rim, rim), specs=[SMEM, VMEM]
    )(spot, whole)
    low = ring(to_next, 1)
    high = ring(to_prev, -1)
    far = exchange(far_send, FAR_GROUPS)
    near_send = call(near_kernel, slots, specs=[SMEM] + [VMEM] * 2)(spot, pooled, far)
    near = exchange(near_send, NEAR_GROUPS)
    rim_grad = shape(LEAF + COUNT[0], 2 * SPAN)
    attended, query_grad, centre, to_prev, to_next, near_send = call(
        attend_kernel,
        (
            shape(TOKENS, SPAN),
            shape(TOKENS, SPAN),
            shape(TOKENS, 2 * SPAN, kind=F32),
            rim_grad,
            rim_grad,
            slots,
        ),
        [
            pltpu.VMEM((2 * LEAF + TOKENS, HEAD_DIM), BF16),
            pltpu.VMEM((2 * LEAF + TOKENS, HEAD_DIM), BF16),
            pltpu.VMEM((2 * LEAF + TOKENS, HEAD_DIM), F32),
            pltpu.VMEM((2 * LEAF + TOKENS, HEAD_DIM), F32),
            pltpu.VMEM((COARSE, HEAD_DIM), BF16),
            pltpu.VMEM((COARSE, HEAD_DIM), BF16),
        ],
        [SMEM] + [VMEM] * 4,
    )(spot, whole, low, high, near)
    from_next = ring(to_prev, -1)
    from_prev = ring(to_next, 1)
    near = exchange(near_send, NEAR_GROUPS)
    far_send = call(far_kernel, far_slots, specs=[SMEM, VMEM])(spot, near)
    far = exchange(far_send, FAR_GROUPS)
    key_grad, value_grad = call(
        finish_kernel,
        (shape(TOKENS, SPAN), shape(TOKENS, SPAN)),
        [pltpu.VMEM((COUNT[0], 2 * SPAN), BF16)],
        [SMEM] + [VMEM] * 5,
    )(spot, centre, from_prev, from_next, near, far)
    return attended, query_grad, key_grad, value_grad


def solution(mesh):
    spec = P(("context", "head"), None)
    out = P("context", "head")
    return jax.shard_map(
        body, mesh=mesh, in_specs=(spec,) * 4, out_specs=(out,) * 4, check_vma=False
    )
```

```python
import math

import jax
import jax.numpy as jnp
from jax import lax
from jax.experimental import pallas as pl
from jax.experimental.pallas import tpu as pltpu
from jax.sharding import PartitionSpec as P

HEAD_DIM = 128
LEAF = 256
RATIO = 16
TOKENS = 512
SPAN = 256
SHARES = 8
SHARE = 64
LEVELS = 6
OWN = 64
COUNT = [32 >> level for level in range(LEVELS)]
START = [64 - (64 >> level) for level in range(LEVELS)]
PEERS = 64
SLOT = 8
SLOTS = PEERS * SLOT
FAR = 4 * 32
COARSE = FAR + 2 * COUNT[1] + COUNT[0]
F32 = jnp.float32
BF16 = jnp.bfloat16
VMEM = pl.BlockSpec(memory_space=pltpu.VMEM)
SMEM = pl.BlockSpec(memory_space=pltpu.SMEM)
ANY = pl.BlockSpec(memory_space=pl.ANY)
LIMIT = pltpu.CompilerParams(vmem_limit_bytes=24 * 1024 * 1024)
NN = ((1,), (0,))
NT = ((1,), (1,))


def dot(left, right, over):
    return lax.dot_general(left, right, (over, ((), ())), preferred_element_type=F32)


def call(kernel, out_shape, scratch=(), specs=None, count=1):
    return pl.pallas_call(
        kernel,
        out_shape=out_shape,
        in_specs=specs or [VMEM] * count,
        out_specs=jax.tree.map(lambda _: VMEM, out_shape),
        scratch_shapes=scratch,
        compiler_params=LIMIT,
    )


def shape(*sizes, kind=BF16):
    return jax.ShapeDtypeStruct(sizes, kind)


def grid(rows, columns):
    return (
        lax.broadcasted_iota(jnp.int32, (rows, columns), 0),
        lax.broadcasted_iota(jnp.int32, (rows, columns), 1),
    )


def ones(hit):
    return jnp.where(hit, 1.0, 0.0).astype(BF16)


def pick(index, cases, last):
    result = last
    for bound, value in reversed(cases):
        result = jnp.where(index < bound, value, result)
    return result


def slot_row(offset, row):
    count = pick(offset, [(4, 0), (8, COUNT[2]), (16, COUNT[3]), (32, COUNT[4])], COUNT[5])
    start = pick(offset, [(8, START[2]), (16, START[3]), (32, START[4])], START[5])
    return row < count, start + row


def slot_of(row):
    offset = pick(row, [(32, 4 + (row >> 3)), (64, row >> 2), (96, (row >> 1) - 16)], row - 64)
    return offset, pick(row, [(32, row & 7), (64, row & 3), (96, row & 1)], 0)


def pack_kernel(key, value, query, cotangent, packed, rows, held, arrived, left):
    incoming = [
        pltpu.make_async_copy(source, rows.at[part], arrived.at[part])
        for part, source in enumerate((key, value, query, cotangent))
    ]
    for copy in incoming:
        copy.start()
    outgoing = []
    for part, copy in enumerate(incoming):
        copy.wait()
        place = slice(part * SHARE, (part + 1) * SHARE)
        for share in range(SHARES):
            held[share, place, :] = rows[part, :, share * SPAN : (share + 1) * SPAN]
        outgoing.append(
            pltpu.make_async_copy(held.at[:, place, :], packed.at[:, place, :], left.at[part])
        )
        outgoing[-1].start()
    for copy in outgoing:
        copy.wait()


def pack(*sources):
    return pl.pallas_call(
        pack_kernel,
        out_shape=shape(SHARES, 4 * SHARE, SPAN),
        in_specs=[ANY] * 4,
        out_specs=ANY,
        scratch_shapes=[
            pltpu.VMEM((4, SHARE, SHARES * SPAN), BF16),
            pltpu.VMEM((SHARES, 4 * SHARE, SPAN), BF16),
            pltpu.SemaphoreType.DMA((4,)),
            pltpu.SemaphoreType.DMA((4,)),
        ],
        compiler_params=pltpu.CompilerParams(vmem_limit_bytes=60 * 1024 * 1024),
    )(*sources)


def pool_kernel(spot, whole, level_one, slots, to_next, to_prev):
    row, token = grid(OWN, TOKENS)
    weight = jnp.zeros((OWN, TOKENS), F32)
    for level in range(LEVELS):
        shift = 4 + level
        hit = row == START[level] + lax.shift_right_logical(token, shift)
        weight = jnp.where(hit, 1.0 / (1 << shift), weight)
    weight = weight.astype(BF16)
    row, column = grid(SLOTS, OWN)
    valid, source = slot_row((row >> 3) ^ spot[0], row & 7)
    spread = ones(valid & (column == source))
    for part in range(2):
        rows = whole[:, part * SHARE : (part + 1) * SHARE, :].reshape(TOKENS, SPAN)
        means = dot(weight, rows, NN).astype(BF16)
        columns = slice(part * SPAN, (part + 1) * SPAN)
        level_one[:, columns] = means[START[1] : START[1] + COUNT[1]]
        place = slice(TOKENS + part * COUNT[0], TOKENS + (part + 1) * COUNT[0])
        to_next[place, :] = means[: COUNT[0]]
        to_prev[place, :] = means[: COUNT[0]]
        slots[:, :, columns] = dot(spread, means, NN).astype(BF16).reshape(PEERS, SLOT, SPAN)
    to_prev[:TOKENS, :] = whole[: SHARES // 2, : 2 * SHARE, :].reshape(TOKENS, SPAN)
    to_next[:TOKENS, :] = whole[SHARES // 2 :, : 2 * SHARE, :].reshape(TOKENS, SPAN)


def select_kernel(spot, _after, gather, scatter):
    row, column = grid(FAR, SLOTS)
    offset, place = slot_of(row)
    gather[...] = ones(column == (offset ^ spot[0]) * SLOT + place)
    row, column = grid(SLOTS, FAR)
    offset, place = slot_of(column)
    scatter[...] = ones(row == (offset ^ spot[0]) * SLOT + place)


def part_rows(part):
    return slice(part * SHARE, (part + 1) * SHARE)


def part_columns(part, head):
    return slice(part * SPAN + head * HEAD_DIM, part * SPAN + (head + 1) * HEAD_DIM)


def load(whole, part, block, columns):
    half = SHARES // 2
    return whole[block * half : (block + 1) * half, part_rows(part), columns].reshape(LEAF, HEAD_DIM)


def ext(whole, low, high, part, columns, store):
    half = SHARES // 2
    for place, rim in ((0, low), (LEAF + TOKENS, high)):
        store[place : place + LEAF, :] = (
            rim[:TOKENS, columns]
            .reshape(half, 2 * SHARE, HEAD_DIM)[:, part_rows(part)]
            .reshape(LEAF, HEAD_DIM)
        )
    store[LEAF : LEAF + TOKENS, :] = whole[:, part_rows(part), columns].reshape(TOKENS, HEAD_DIM)


def near_scores(spot, keys, query, block):
    window = slice(block * LEAF, block * LEAF + 3 * LEAF)
    near = dot(keys[window, :], query, NT) * (HEAD_DIM ** (-0.5) * math.log2(math.e))
    if block == 0:
        bias = jnp.where(spot[0] == 0, -1e30, 0.0).astype(F32)
        return jnp.concatenate([near[:LEAF] + bias, near[LEAF:]], axis=0)
    bias = jnp.where(spot[0] == spot[1] - 1, -1e30, 0.0).astype(F32)
    return jnp.concatenate([near[: 2 * LEAF], near[2 * LEAF :] + bias], axis=0)


def forward_kernel(
    spot, whole, low, high, slots, two, three, gather, scatter,
    attended, far_query, stats, slots_back, two_back, three_back, zero_back,
    keys, values, coarse,
):
    factor = HEAD_DIM ** (-0.5)
    binary = factor * math.log2(math.e)
    even = (spot[0] & 1) == 0
    for rim, flag in ((high, even), (low, jnp.logical_not(even))):

        @pl.when(flag)
        def _():
            for part in range(2):
                summary = slice(TOKENS + part * COUNT[0], TOKENS + (part + 1) * COUNT[0])
                coarse[COARSE - COUNT[0] :, part * SPAN : (part + 1) * SPAN] = rim[summary, :]

    coarse[:FAR, :] = dot(gather[...], slots[...].reshape(SLOTS, 2 * SPAN), NN).astype(BF16)
    coarse[FAR : FAR + COUNT[1], :] = two[...]
    coarse[FAR + COUNT[1] : FAR + 2 * COUNT[1], :] = three[...]
    heads, units = range(2), [(head, block) for head in range(2) for block in range(2)]
    columns = [slice(head * HEAD_DIM, (head + 1) * HEAD_DIM) for head in heads]
    for head in heads:
        ext(whole, low, high, 0, columns[head], keys.at[head])
        ext(whole, low, high, 1, columns[head], values.at[head])
    far_key = [coarse[:, part_columns(0, head)] for head in heads]
    far_value = [coarse[:, part_columns(1, head)] for head in heads]
    value_t = [jnp.transpose(values[head]) for head in heads]
    far_key_t = [jnp.transpose(far_key[head]) for head in heads]
    far_value_t = [jnp.transpose(far_value[head]) for head in heads]
    query = [load(whole, 2, block, columns[head]) for head, block in units]
    grad = [load(whole, 3, block, columns[head]) for head, block in units]
    state = []
    for unit, (head, block) in enumerate(units):
        near = near_scores(spot, keys.at[head], query[unit], block)
        far = dot(far_key[head], query[unit], NT) * binary + math.log2(RATIO)
        slope = dot(far_value[head], grad[unit], NT)
        state.append((near, far, slope))
    lows = []
    for unit, (head, block) in enumerate(units):
        near, far, slope = state[unit]
        top = jnp.maximum(jnp.max(near, axis=0, keepdims=True), jnp.max(far, axis=0, keepdims=True))
        near = jnp.exp2(near - top)
        far = jnp.exp2(far - top)
        total = jnp.sum(near, axis=0, keepdims=True) + jnp.sum(far, axis=0, keepdims=True)
        inverse = 1.0 / total
        far = far * inverse
        far_low = far.astype(BF16)
        near_low = (near * inverse).astype(BF16)
        stats[unit : unit + 1, :] = top
        stats[4 + unit : 5 + unit, :] = inverse
        window = slice(block * LEAF, block * LEAF + 3 * LEAF)
        mixed_t = dot(value_t[head][:, window], near_low, NN) + dot(far_value_t[head], far_low, NN)
        lows.append((far, far_low, mixed_t, slope))
    key_grads, value_grads = [], []
    for unit, (head, block) in enumerate(units):
        far, far_low, mixed_t, slope = lows[unit]
        grad_t = jnp.transpose(grad[unit].astype(F32))
        delta = jnp.sum(grad_t * mixed_t, axis=0, keepdims=True)
        stats[8 + unit : 9 + unit, :] = delta
        score = (far * (slope - delta)).astype(BF16)
        far_query[unit] = dot(far_key_t[head], score, NN)
        rows = slice(block * LEAF, (block + 1) * LEAF)
        attended[rows, columns[head]] = jnp.transpose(mixed_t).astype(BF16)
        key_grads.append(dot(score, query[unit], NN))
        value_grads.append(dot(far_low, grad[unit], NN))
    for head in heads:
        key_grad = ((key_grads[2 * head] + key_grads[2 * head + 1]) * factor).astype(BF16)
        value_grad = (value_grads[2 * head] + value_grads[2 * head + 1]).astype(BF16)
        for part, far_grad in ((0, key_grad), (1, value_grad)):
            place = part_columns(part, head)
            two_back[:, place] = far_grad[FAR : FAR + COUNT[1]]
            three_back[:, place] = far_grad[FAR + COUNT[1] : FAR + 2 * COUNT[1]]
            zero_back[:, place] = far_grad[FAR + 2 * COUNT[1] :]
            slots_back[:, :, place] = (
                dot(scatter[...], far_grad[:FAR], NN).astype(BF16).reshape(PEERS, SLOT, HEAD_DIM)
            )


def backward_kernel(
    spot, whole, low, high, stats, far_query, level_zero,
    query_grad, centre, to_prev, to_next,
    keys, values, key_grad, value_grad,
):
    factor = HEAD_DIM ** (-0.5)
    for head in range(2):
        columns = slice(head * HEAD_DIM, (head + 1) * HEAD_DIM)
        ext(whole, low, high, 0, columns, keys)
        ext(whole, low, high, 1, columns, values)
        key_t = jnp.transpose(keys[...])
        for block in range(2):
            unit = 2 * head + block
            query = load(whole, 2, block, columns)
            grad = load(whole, 3, block, columns)
            window = slice(block * LEAF, block * LEAF + 3 * LEAF)
            near = near_scores(spot, keys, query, block)
            near = jnp.exp2(near - stats[unit : unit + 1, :]) * stats[4 + unit : 5 + unit, :]
            near_low = near.astype(BF16)
            slope = dot(values[window, :], grad, NT) - stats[8 + unit : 9 + unit, :]
            score = (near * slope).astype(BF16)
            query_t = dot(key_t[:, window], score, NN) + far_query[unit]
            query_grad[block * LEAF : (block + 1) * LEAF, columns] = jnp.transpose(
                query_t * factor
            ).astype(BF16)
            near_key_grad = dot(score, query, NN) * factor
            near_value_grad = dot(near_low, grad, NN)
            if block == 0:
                key_grad[: 3 * LEAF, :] = near_key_grad
                value_grad[: 3 * LEAF, :] = near_value_grad
            else:
                key_grad[LEAF : 3 * LEAF, :] += near_key_grad[: 2 * LEAF]
                value_grad[LEAF : 3 * LEAF, :] += near_value_grad[: 2 * LEAF]
                key_grad[3 * LEAF :, :] = near_key_grad[2 * LEAF :]
                value_grad[3 * LEAF :, :] = near_value_grad[2 * LEAF :]
        for part, store in ((0, key_grad), (1, value_grad)):
            place = part_columns(part, head)
            to_prev[:LEAF, place] = store[:LEAF, :].astype(BF16)
            centre[:, place] = store[LEAF : LEAF + TOKENS, :]
            to_next[:LEAF, place] = store[LEAF + TOKENS :, :].astype(BF16)
    to_prev[LEAF:, :] = level_zero[...]
    to_next[LEAF:, :] = level_zero[...]


def gather_kernel(
    spot, centre, from_prev, from_next, two, three, total, weight, level_zero
):
    even = (spot[0] & 1) == 0
    for rim, flag in ((from_next, even), (from_prev, jnp.logical_not(even))):

        @pl.when(flag)
        def _():
            level_zero[...] = rim[LEAF:, :]

    token, column = grid(TOKENS, COUNT[0])
    own = jnp.where((token >> 4) == column, 1.0 / RATIO, 0.0).astype(BF16)
    spread = centre[...] + dot(own, level_zero[...], NN)
    token, column = grid(TOKENS, COUNT[1])
    own = jnp.where((token >> 5) == column, 1.0 / (2 * RATIO), 0.0).astype(BF16)
    spread = spread + dot(own, two[...], NN) + dot(own, three[...], NN)
    total[:LEAF, :] = spread[:LEAF] + from_prev[:LEAF, :].astype(F32)
    total[LEAF:, :] = spread[LEAF:] + from_next[:LEAF, :].astype(F32)
    token, column = grid(TOKENS, SLOTS)
    valid, source = slot_row((column >> 3) ^ spot[0], column & 7)
    result = jnp.zeros((TOKENS, SLOTS), F32)
    for level in range(2, LEVELS):
        shift = 4 + level
        hit = valid & (source == START[level] + (token >> shift))
        result = jnp.where(hit, 1.0 / (1 << shift), result)
    weight[...] = result.astype(BF16)


def finish_kernel(total, weight, slots, key_grad, value_grad):
    rows = slots[...].reshape(SLOTS, 2 * SPAN)
    result = (total[...] + dot(weight[...], rows, NN)).astype(BF16)
    key_grad[...] = result[:, :SPAN]
    value_grad[...] = result[:, SPAN:]


def body(query, key, value, cotangent):
    devices = lax.axis_size("context")
    position = lax.axis_index("context")
    spot = jnp.stack([position, jnp.int32(devices)])

    def ring(block, step):
        pairs = [(source, (source + step) % devices) for source in range(devices)]
        return lax.ppermute(block, "context", pairs)

    def partner(block, offset):
        pairs = [(source, source ^ offset) for source in range(devices)]
        return lax.ppermute(block, "context", pairs)

    whole = lax.all_to_all(pack(key, value, query, cotangent), "head", 0, 0)
    slots = shape(PEERS, SLOT, 2 * SPAN)
    rim = shape(TOKENS + 2 * COUNT[0], SPAN)
    one = shape(COUNT[1], 2 * SPAN)
    level_one, slots_out, to_next, to_prev = call(
        pool_kernel, (one, slots, rim, rim), specs=[SMEM, VMEM]
    )(spot, whole)
    slots_in = lax.all_to_all(slots_out, "context", 0, 0)
    low = ring(to_next, 1)
    high = ring(to_prev, -1)
    two = partner(level_one, 2)
    three = partner(level_one, 3)
    gather, scatter = call(
        select_kernel, (shape(FAR, SLOTS), shape(SLOTS, FAR)), specs=[SMEM, VMEM]
    )(spot, level_one)
    span = 2 * LEAF + TOKENS
    attended, far_query, stats, slots_back, two_back, three_back, zero_back = call(
        forward_kernel,
        (
            shape(TOKENS, SPAN),
            shape(4, HEAD_DIM, LEAF, kind=F32),
            shape(16, LEAF, kind=F32),
            slots,
            one,
            one,
            shape(COUNT[0], 2 * SPAN),
        ),
        [pltpu.VMEM((2, span, HEAD_DIM), BF16)] * 2 + [pltpu.VMEM((COARSE, 2 * SPAN), BF16)],
        [SMEM] + [VMEM] * 8,
    )(spot, whole, low, high, slots_in, two, three, gather, scatter)
    slots_back = lax.all_to_all(slots_back, "context", 0, 0)
    two_back = partner(two_back, 2)
    three_back = partner(three_back, 3)
    rim_grad = shape(LEAF + COUNT[0], 2 * SPAN)
    query_grad, centre, to_prev, to_next = call(
        backward_kernel,
        (shape(TOKENS, SPAN), shape(TOKENS, 2 * SPAN, kind=F32), rim_grad, rim_grad),
        [pltpu.VMEM((span, HEAD_DIM), BF16)] * 2 + [pltpu.VMEM((span, HEAD_DIM), F32)] * 2,
        [SMEM] + [VMEM] * 6,
    )(spot, whole, low, high, stats, far_query, zero_back)
    from_next = ring(to_prev, -1)
    from_prev = ring(to_next, 1)
    total, weight = call(
        gather_kernel,
        (shape(TOKENS, 2 * SPAN, kind=F32), shape(TOKENS, SLOTS)),
        [pltpu.VMEM((COUNT[0], 2 * SPAN), BF16)],
        [SMEM] + [VMEM] * 5,
    )(spot, centre, from_prev, from_next, two_back, three_back)
    key_grad, value_grad = call(
        finish_kernel, (shape(TOKENS, SPAN), shape(TOKENS, SPAN)), count=3
    )(total, weight, slots_back)
    return attended, query_grad, key_grad, value_grad


def solution(mesh):
    spec = P(("context", "head"), None)
    out = P("context", "head")
    return jax.shard_map(
        body, mesh=mesh, in_specs=(spec,) * 4, out_specs=(out,) * 4, check_vma=False
    )
```

```python
import math

import jax
import jax.numpy as jnp
from jax import lax
from jax.experimental import pallas as pl
from jax.experimental.pallas import tpu as pltpu
from jax.sharding import PartitionSpec as P

HEAD_DIM = 128
LEAF = 256
RATIO = 16
TOKENS = 512
SPAN = 256
SHARES = 8
SHARE = 64
LEVELS = 6
OWN = 64
COUNT = [32 >> level for level in range(LEVELS)]
START = [64 - (64 >> level) for level in range(LEVELS)]
FAR_PEERS = 16
FAR_ROWS = 8
FAR = FAR_PEERS * FAR_ROWS
NEAR_PEERS = 4
NEAR_BITS = 2
NEAR_ROWS = 48
HELD = 32
NEAR = NEAR_PEERS * NEAR_ROWS
COARSE = COUNT[0] + NEAR_PEERS * HELD + 2 * COUNT[1]
F32 = jnp.float32
BF16 = jnp.bfloat16
VMEM = pl.BlockSpec(memory_space=pltpu.VMEM)
SMEM = pl.BlockSpec(memory_space=pltpu.SMEM)
ANY = pl.BlockSpec(memory_space=pl.ANY)
LIMIT = pltpu.CompilerParams(vmem_limit_bytes=24 * 1024 * 1024)
NN = ((1,), (0,))
NT = ((1,), (1,))


def dot(left, right, over):
    return lax.dot_general(left, right, (over, ((), ())), preferred_element_type=F32)


def call(kernel, out_shape, scratch=(), specs=None, count=1, cost=None):
    return pl.pallas_call(
        kernel,
        out_shape=out_shape,
        in_specs=specs or [VMEM] * count,
        out_specs=jax.tree.map(lambda _: VMEM, out_shape),
        scratch_shapes=scratch,
        compiler_params=LIMIT,
        cost_estimate=cost,
    )


def shape(*sizes, kind=BF16):
    return jax.ShapeDtypeStruct(sizes, kind)


def grid(rows, columns):
    return (
        lax.broadcasted_iota(jnp.int32, (rows, columns), 0),
        lax.broadcasted_iota(jnp.int32, (rows, columns), 1),
    )


def ones(hit):
    return jnp.where(hit, 1.0, 0.0).astype(BF16)


def pick(index, cases, last):
    result = last
    for bound, value in reversed(cases):
        result = jnp.where(index < bound, value, result)
    return result


def far_slot(offset, row):
    count = pick(offset, [(1, 0), (2, COUNT[2]), (4, COUNT[3]), (8, COUNT[4])], COUNT[5])
    start = pick(offset, [(2, START[2]), (4, START[3]), (8, START[4])], START[5])
    return row < count, start + row


def near_slot(offset, row):
    return (offset >= 2) & (row >= HELD), START[1] + row - HELD


def held_slot(row):
    offset = pick(row, [(8, 1), (16, row >> 2), (24, (row >> 1) - 4)], row - 16)
    return row < HELD, offset, pick(row, [(8, row), (16, row & 3), (24, row & 1)], 0)


def near_place(index):
    slot = pick(index, [(NEAR_ROWS, 0), (2 * NEAR_ROWS, 1), (3 * NEAR_ROWS, 2)], 3)
    return slot, index - slot * NEAR_ROWS


def pack_kernel(key, value, query, cotangent, packed, rows, held, arrived, left):
    incoming = [
        pltpu.make_async_copy(source, rows.at[part], arrived.at[part])
        for part, source in enumerate((key, value, query, cotangent))
    ]
    for copy in incoming:
        copy.start()
    outgoing = []
    for part, copy in enumerate(incoming):
        copy.wait()
        place = slice(part * SHARE, (part + 1) * SHARE)
        for share in range(SHARES):
            held[share, place, :] = rows[part, :, share * SPAN : (share + 1) * SPAN]
        outgoing.append(
            pltpu.make_async_copy(held.at[:, place, :], packed.at[:, place, :], left.at[part])
        )
        outgoing[-1].start()
    for copy in outgoing:
        copy.wait()


def pack(*sources):
    return pl.pallas_call(
        pack_kernel,
        out_shape=shape(SHARES, 4 * SHARE, SPAN),
        in_specs=[ANY] * 4,
        out_specs=ANY,
        scratch_shapes=[
            pltpu.VMEM((4, SHARE, SHARES * SPAN), BF16),
            pltpu.VMEM((SHARES, 4 * SHARE, SPAN), BF16),
            pltpu.SemaphoreType.DMA((4,)),
            pltpu.SemaphoreType.DMA((4,)),
        ],
        compiler_params=pltpu.CompilerParams(vmem_limit_bytes=60 * 1024 * 1024),
    )(*sources)


def pool_kernel(spot, whole, pooled, far_send, to_next, to_prev):
    row, token = grid(OWN, TOKENS)
    weight = jnp.zeros((OWN, TOKENS), F32)
    for level in range(LEVELS):
        shift = 4 + level
        hit = row == START[level] + lax.shift_right_logical(token, shift)
        weight = jnp.where(hit, 1.0 / (1 << shift), weight)
    weight = weight.astype(BF16)
    row, column = grid(FAR, OWN)
    valid, source = far_slot((row >> 3) ^ (spot[0] >> NEAR_BITS), row & 7)
    spread = ones(valid & (column == source))
    for part in range(2):
        rows = whole[:, part * SHARE : (part + 1) * SHARE, :].reshape(TOKENS, SPAN)
        means = dot(weight, rows, NN).astype(BF16)
        columns = slice(part * SPAN, (part + 1) * SPAN)
        pooled[:, columns] = means
        place = slice(TOKENS + part * COUNT[0], TOKENS + (part + 1) * COUNT[0])
        to_next[place, :] = means[: COUNT[0]]
        to_prev[place, :] = means[: COUNT[0]]
        far_send[:, :, columns] = dot(spread, means, NN).astype(BF16).reshape(FAR_PEERS, FAR_ROWS, SPAN)
    to_prev[:TOKENS, :] = whole[: SHARES // 2, : 2 * SHARE, :].reshape(TOKENS, SPAN)
    to_next[:TOKENS, :] = whole[SHARES // 2 :, : 2 * SHARE, :].reshape(TOKENS, SPAN)


def own_kernel(spot, pooled, _low, _high, own, gather):
    far_at, near_at = spot[0] >> NEAR_BITS, spot[0] & (NEAR_PEERS - 1)
    index, column = grid(NEAR, OWN)
    slot, inside = near_place(index)
    valid, source = near_slot(slot ^ near_at, inside)
    own[...] = dot(ones(valid & (column == source)), pooled[...], NN)
    index, column = grid(NEAR, FAR)
    slot, inside = near_place(index)
    valid, offset, place = held_slot(inside)
    gather[...] = ones(valid & (column == (offset ^ far_at) * FAR_ROWS + place))


def near_kernel(own, gather, far, near_send):
    held = dot(gather[...], far[...].reshape(FAR, 2 * SPAN), NN)
    near_send[...] = (own[...] + held).astype(BF16).reshape(NEAR_PEERS, NEAR_ROWS, 2 * SPAN)


def far_send_kernel(scatter, near, far_send):
    far_send[...] = (
        dot(scatter[...], near[...].reshape(NEAR, 2 * SPAN), NN)
        .astype(BF16)
        .reshape(FAR_PEERS, FAR_ROWS, 2 * SPAN)
    )


def part_rows(part):
    return slice(part * SHARE, (part + 1) * SHARE)


def part_columns(part, head):
    return slice(part * SPAN + head * HEAD_DIM, part * SPAN + (head + 1) * HEAD_DIM)


def load(whole, part, block, columns):
    half = SHARES // 2
    return whole[block * half : (block + 1) * half, part_rows(part), columns].reshape(LEAF, HEAD_DIM)


def ext(whole, low, high, part, columns, store):
    half = SHARES // 2
    for place, rim in ((0, low), (LEAF + TOKENS, high)):
        store[place : place + LEAF, :] = (
            rim[:TOKENS, columns]
            .reshape(half, 2 * SHARE, HEAD_DIM)[:, part_rows(part)]
            .reshape(LEAF, HEAD_DIM)
        )
    store[LEAF : LEAF + TOKENS, :] = whole[:, part_rows(part), columns].reshape(TOKENS, HEAD_DIM)


def near_scores(spot, keys, query, block):
    window = slice(block * LEAF, block * LEAF + 3 * LEAF)
    near = dot(keys[window, :], query, NT) * (HEAD_DIM ** (-0.5) * math.log2(math.e))
    if block == 0:
        bias = jnp.where(spot[0] == 0, -1e30, 0.0).astype(F32)
        return jnp.concatenate([near[:LEAF] + bias, near[LEAF:]], axis=0)
    bias = jnp.where(spot[0] == spot[1] - 1, -1e30, 0.0).astype(F32)
    return jnp.concatenate([near[: 2 * LEAF], near[2 * LEAF :] + bias], axis=0)


def forward_kernel(
    spot, whole, low, high, near_rows,
    attended, far_query, stats, near_send, zero_back,
    keys, values, coarse,
):
    factor = HEAD_DIM ** (-0.5)
    binary = factor * math.log2(math.e)
    even = (spot[0] & 1) == 0
    for rim, flag in ((high, even), (low, jnp.logical_not(even))):

        @pl.when(flag)
        def _():
            for part in range(2):
                summary = slice(TOKENS + part * COUNT[0], TOKENS + (part + 1) * COUNT[0])
                coarse[COARSE - COUNT[0] :, part * SPAN : (part + 1) * SPAN] = rim[summary, :]

    near_at = spot[0] & (NEAR_PEERS - 1)
    for slot in range(NEAR_PEERS):
        coarse[slot * HELD : (slot + 1) * HELD, :] = near_rows[slot, :HELD, :]
    first = NEAR_PEERS * HELD
    for offset in (2, 3):
        start = first + (offset - 2) * COUNT[1]
        coarse[start : start + COUNT[1], :] = near_rows[near_at ^ offset, HELD:, :]
    heads, units = range(2), [(head, block) for head in range(2) for block in range(2)]
    columns = [slice(head * HEAD_DIM, (head + 1) * HEAD_DIM) for head in heads]
    for head in heads:
        ext(whole, low, high, 0, columns[head], keys.at[head])
        ext(whole, low, high, 1, columns[head], values.at[head])
    far_key = [coarse[:, part_columns(0, head)] for head in heads]
    far_value = [coarse[:, part_columns(1, head)] for head in heads]
    value_t = [jnp.transpose(values[head]) for head in heads]
    far_key_t = [jnp.transpose(far_key[head]) for head in heads]
    far_value_t = [jnp.transpose(far_value[head]) for head in heads]
    query = [load(whole, 2, block, columns[head]) for head, block in units]
    grad = [load(whole, 3, block, columns[head]) for head, block in units]
    state = []
    for unit, (head, block) in enumerate(units):
        near = near_scores(spot, keys.at[head], query[unit], block)
        far = dot(far_key[head], query[unit], NT) * binary + math.log2(RATIO)
        slope = dot(far_value[head], grad[unit], NT)
        state.append((near, far, slope))
    lows = []
    for unit, (head, block) in enumerate(units):
        near, far, slope = state[unit]
        top = jnp.maximum(jnp.max(near, axis=0, keepdims=True), jnp.max(far, axis=0, keepdims=True))
        near = jnp.exp2(near - top)
        far = jnp.exp2(far - top)
        total = jnp.sum(near, axis=0, keepdims=True) + jnp.sum(far, axis=0, keepdims=True)
        inverse = 1.0 / total
        far = far * inverse
        far_low = far.astype(BF16)
        near_low = (near * inverse).astype(BF16)
        stats[unit : unit + 1, :] = top
        stats[4 + unit : 5 + unit, :] = inverse
        window = slice(block * LEAF, block * LEAF + 3 * LEAF)
        mixed_t = dot(value_t[head][:, window], near_low, NN) + dot(far_value_t[head], far_low, NN)
        lows.append((far, far_low, mixed_t, slope))
    key_grads, value_grads = [], []
    for unit, (head, block) in enumerate(units):
        far, far_low, mixed_t, slope = lows[unit]
        grad_t = jnp.transpose(grad[unit].astype(F32))
        delta = jnp.sum(grad_t * mixed_t, axis=0, keepdims=True)
        stats[8 + unit : 9 + unit, :] = delta
        score = (far * (slope - delta)).astype(BF16)
        far_query[unit] = dot(far_key_t[head], score, NN)
        rows = slice(block * LEAF, (block + 1) * LEAF)
        attended[rows, columns[head]] = jnp.transpose(mixed_t).astype(BF16)
        key_grads.append(dot(score, query[unit], NN))
        value_grads.append(dot(far_low, grad[unit], NN))
    for head in heads:
        key_grad = ((key_grads[2 * head] + key_grads[2 * head + 1]) * factor).astype(BF16)
        value_grad = (value_grads[2 * head] + value_grads[2 * head + 1]).astype(BF16)
        for part, far_grad in ((0, key_grad), (1, value_grad)):
            place = part_columns(part, head)
            zero_back[:, place] = far_grad[first + 2 * COUNT[1] :]
            for slot in range(NEAR_PEERS):
                near_send[slot, :HELD, place] = far_grad[slot * HELD : (slot + 1) * HELD]
            for offset in (0, 1):
                near_send[near_at ^ offset, HELD:, place] = jnp.zeros((COUNT[1], HEAD_DIM), BF16)
            for offset in (2, 3):
                start = first + (offset - 2) * COUNT[1]
                near_send[near_at ^ offset, HELD:, place] = far_grad[start : start + COUNT[1]]


def backward_kernel(
    spot, whole, low, high, stats, far_query, level_zero,
    query_grad, centre, to_prev, to_next, scatter,
    keys, values, key_grad, value_grad,
):
    factor = HEAD_DIM ** (-0.5)
    for head in range(2):
        columns = slice(head * HEAD_DIM, (head + 1) * HEAD_DIM)
        ext(whole, low, high, 0, columns, keys)
        ext(whole, low, high, 1, columns, values)
        key_t = jnp.transpose(keys[...])
        for block in range(2):
            unit = 2 * head + block
            query = load(whole, 2, block, columns)
            grad = load(whole, 3, block, columns)
            window = slice(block * LEAF, block * LEAF + 3 * LEAF)
            near = near_scores(spot, keys, query, block)
            near = jnp.exp2(near - stats[unit : unit + 1, :]) * stats[4 + unit : 5 + unit, :]
            near_low = near.astype(BF16)
            slope = dot(values[window, :], grad, NT) - stats[8 + unit : 9 + unit, :]
            score = (near * slope).astype(BF16)
            query_t = dot(key_t[:, window], score, NN) + far_query[unit]
            query_grad[block * LEAF : (block + 1) * LEAF, columns] = jnp.transpose(
                query_t * factor
            ).astype(BF16)
            near_key_grad = dot(score, query, NN) * factor
            near_value_grad = dot(near_low, grad, NN)
            if block == 0:
                key_grad[: 3 * LEAF, :] = near_key_grad
                value_grad[: 3 * LEAF, :] = near_value_grad
            else:
                key_grad[LEAF : 3 * LEAF, :] += near_key_grad[: 2 * LEAF]
                value_grad[LEAF : 3 * LEAF, :] += near_value_grad[: 2 * LEAF]
                key_grad[3 * LEAF :, :] = near_key_grad[2 * LEAF :]
                value_grad[3 * LEAF :, :] = near_value_grad[2 * LEAF :]
        for part, store in ((0, key_grad), (1, value_grad)):
            place = part_columns(part, head)
            to_prev[:LEAF, place] = store[:LEAF, :].astype(BF16)
            centre[:, place] = store[LEAF : LEAF + TOKENS, :]
            to_next[:LEAF, place] = store[LEAF + TOKENS :, :].astype(BF16)
    to_prev[LEAF:, :] = level_zero[...]
    to_next[LEAF:, :] = level_zero[...]
    row, column = grid(FAR, NEAR)
    _, inside = near_place(column)
    valid, offset, place = held_slot(inside)
    hit = valid & (offset == ((row >> 3) ^ (spot[0] >> NEAR_BITS))) & (place == (row & 7))
    scatter[...] = ones(hit)


def gather_kernel(
    spot, centre, from_prev, from_next, near, total, weight, level_zero
):
    even = (spot[0] & 1) == 0
    for rim, flag in ((from_next, even), (from_prev, jnp.logical_not(even))):

        @pl.when(flag)
        def _():
            level_zero[...] = rim[LEAF:, :]

    token, column = grid(TOKENS, COUNT[0])
    own = jnp.where((token >> 4) == column, 1.0 / RATIO, 0.0).astype(BF16)
    spread = centre[...] + dot(own, level_zero[...], NN)
    token, column = grid(TOKENS, COUNT[1])
    own = jnp.where((token >> 5) == column, 1.0 / (2 * RATIO), 0.0).astype(BF16)
    near_at = spot[0] & (NEAR_PEERS - 1)
    for offset in (2, 3):
        spread = spread + dot(own, near[near_at ^ offset, HELD:, :], NN)
    total[:LEAF, :] = spread[:LEAF] + from_prev[:LEAF, :].astype(F32)
    total[LEAF:, :] = spread[LEAF:] + from_next[:LEAF, :].astype(F32)
    token, column = grid(TOKENS, FAR)
    valid, source = far_slot((column >> 3) ^ (spot[0] >> NEAR_BITS), column & 7)
    result = jnp.zeros((TOKENS, FAR), F32)
    for level in range(2, LEVELS):
        shift = 4 + level
        hit = valid & (source == START[level] + (token >> shift))
        result = jnp.where(hit, 1.0 / (1 << shift), result)
    weight[...] = result.astype(BF16)


def finish_kernel(total, weight, far, key_grad, value_grad):
    rows = far[...].reshape(FAR, 2 * SPAN)
    result = (total[...] + dot(weight[...], rows, NN)).astype(BF16)
    key_grad[...] = result[:, :SPAN]
    value_grad[...] = result[:, SPAN:]


FAR_GROUPS = [[far * NEAR_PEERS + near for far in range(FAR_PEERS)] for near in range(NEAR_PEERS)]
NEAR_GROUPS = [[far * NEAR_PEERS + near for near in range(NEAR_PEERS)] for far in range(FAR_PEERS)]


def body(query, key, value, cotangent):
    devices = lax.axis_size("context")
    position = lax.axis_index("context")
    spot = jnp.stack([position, jnp.int32(devices)])

    def ring(block, step):
        pairs = [(source, (source + step) % devices) for source in range(devices)]
        return lax.ppermute(block, "context", pairs)

    def exchange(block, groups):
        return lax.all_to_all(block, "context", 0, 0, axis_index_groups=groups)

    whole = lax.all_to_all(pack(key, value, query, cotangent), "head", 0, 0)
    near_slots = shape(NEAR_PEERS, NEAR_ROWS, 2 * SPAN)
    far_slots = shape(FAR_PEERS, FAR_ROWS, 2 * SPAN)
    rim = shape(TOKENS + 2 * COUNT[0], SPAN)
    pooled, far_send, to_next, to_prev = call(
        pool_kernel, (shape(OWN, 2 * SPAN), far_slots, rim, rim), specs=[SMEM, VMEM]
    )(spot, whole)
    low = ring(to_next, 1)
    high = ring(to_prev, -1)
    far = exchange(far_send, FAR_GROUPS)
    own, gather = call(
        own_kernel,
        (shape(NEAR, 2 * SPAN, kind=F32), shape(NEAR, FAR)),
        specs=[SMEM] + [VMEM] * 3,
        cost=pl.CostEstimate(flops=5000000000, bytes_accessed=0, transcendentals=0),
    )(spot, pooled, low, high)
    near = exchange(call(near_kernel, near_slots, count=3)(own, gather, far), NEAR_GROUPS)
    span = 2 * LEAF + TOKENS
    attended, far_query, stats, near_send, zero_back = call(
        forward_kernel,
        (
            shape(TOKENS, SPAN),
            shape(4, HEAD_DIM, LEAF, kind=F32),
            shape(16, LEAF, kind=F32),
            near_slots,
            shape(COUNT[0], 2 * SPAN),
        ),
        [pltpu.VMEM((2, span, HEAD_DIM), BF16)] * 2 + [pltpu.VMEM((COARSE, 2 * SPAN), BF16)],
        [SMEM] + [VMEM] * 4,
    )(spot, whole, low, high, near)
    near = exchange(near_send, NEAR_GROUPS)
    rim_grad = shape(LEAF + COUNT[0], 2 * SPAN)
    query_grad, centre, to_prev, to_next, scatter = call(
        backward_kernel,
        (
            shape(TOKENS, SPAN),
            shape(TOKENS, 2 * SPAN, kind=F32),
            rim_grad,
            rim_grad,
            shape(FAR, NEAR),
        ),
        [pltpu.VMEM((span, HEAD_DIM), BF16)] * 2 + [pltpu.VMEM((span, HEAD_DIM), F32)] * 2,
        [SMEM] + [VMEM] * 6,
        cost=None,
    )(spot, whole, low, high, stats, far_query, zero_back)
    from_next = ring(to_prev, -1)
    from_prev = ring(to_next, 1)
    far = exchange(call(far_send_kernel, far_slots, count=2)(scatter, near), FAR_GROUPS)
    total, weight = call(
        gather_kernel,
        (shape(TOKENS, 2 * SPAN, kind=F32), shape(TOKENS, FAR)),
        [pltpu.VMEM((COUNT[0], 2 * SPAN), BF16)],
        [SMEM] + [VMEM] * 4,
        cost=pl.CostEstimate(flops=5000000000, bytes_accessed=0, transcendentals=0),
    )(spot, centre, from_prev, from_next, near)
    key_grad, value_grad = call(
        finish_kernel, (shape(TOKENS, SPAN), shape(TOKENS, SPAN)), count=3
    )(total, weight, far)
    return attended, query_grad, key_grad, value_grad


def solution(mesh):
    spec = P(("context", "head"), None)
    out = P("context", "head")
    return jax.shard_map(
        body, mesh=mesh, in_specs=(spec,) * 4, out_specs=(out,) * 4, check_vma=False
    )
```

```python
import math

import jax
import jax.numpy as jnp
from jax import lax
from jax.experimental import pallas as pl
from jax.experimental.pallas import tpu as pltpu
from jax.sharding import PartitionSpec as P

HEAD_DIM = 128
LEAF = 256
RATIO = 16
TOKENS = 512
SPAN = 256
SHARES = 8
SHARE = 64
LEVELS = 6
OWN = 64
COUNT = [32 >> level for level in range(LEVELS)]
START = [64 - (64 >> level) for level in range(LEVELS)]
FAR_PEERS = 16
FAR_ROWS = 8
FAR = FAR_PEERS * FAR_ROWS
NEAR_PEERS = 4
NEAR_BITS = 2
NEAR_ROWS = 48
HELD = 32
NEAR = NEAR_PEERS * NEAR_ROWS
COARSE = COUNT[0] + NEAR_PEERS * HELD + 2 * COUNT[1]
F32 = jnp.float32
BF16 = jnp.bfloat16
VMEM = pl.BlockSpec(memory_space=pltpu.VMEM)
SMEM = pl.BlockSpec(memory_space=pltpu.SMEM)
ANY = pl.BlockSpec(memory_space=pl.ANY)
LIMIT = pltpu.CompilerParams(vmem_limit_bytes=24 * 1024 * 1024)
NN = ((1,), (0,))
NT = ((1,), (1,))


def dot(left, right, over):
    return lax.dot_general(left, right, (over, ((), ())), preferred_element_type=F32)


def call(kernel, out_shape, scratch=(), specs=None, count=1, cost=None):
    return pl.pallas_call(
        kernel,
        out_shape=out_shape,
        in_specs=specs or [VMEM] * count,
        out_specs=jax.tree.map(lambda _: VMEM, out_shape),
        scratch_shapes=scratch,
        compiler_params=LIMIT,
        cost_estimate=cost,
    )


def shape(*sizes, kind=BF16):
    return jax.ShapeDtypeStruct(sizes, kind)


def grid(rows, columns):
    return (
        lax.broadcasted_iota(jnp.int32, (rows, columns), 0),
        lax.broadcasted_iota(jnp.int32, (rows, columns), 1),
    )


def ones(hit):
    return jnp.where(hit, 1.0, 0.0).astype(BF16)


def pick(index, cases, last):
    result = last
    for bound, value in reversed(cases):
        result = jnp.where(index < bound, value, result)
    return result


def far_slot(offset, row):
    count = pick(offset, [(1, 0), (2, COUNT[2]), (4, COUNT[3]), (8, COUNT[4])], COUNT[5])
    start = pick(offset, [(2, START[2]), (4, START[3]), (8, START[4])], START[5])
    return row < count, start + row


def near_slot(offset, row):
    return (offset >= 2) & (row >= HELD), START[1] + row - HELD


def held_slot(row):
    offset = pick(row, [(8, 1), (16, row >> 2), (24, (row >> 1) - 4)], row - 16)
    return row < HELD, offset, pick(row, [(8, row), (16, row & 3), (24, row & 1)], 0)


def near_place(index):
    slot = pick(index, [(NEAR_ROWS, 0), (2 * NEAR_ROWS, 1), (3 * NEAR_ROWS, 2)], 3)
    return slot, index - slot * NEAR_ROWS


def pack_kernel(key, value, query, cotangent, packed, rows, held, arrived, left):
    incoming = [
        pltpu.make_async_copy(source, rows.at[part], arrived.at[part])
        for part, source in enumerate((key, value, query, cotangent))
    ]
    for copy in incoming:
        copy.start()
    outgoing = []
    for part, copy in enumerate(incoming):
        copy.wait()
        place = slice(part * SHARE, (part + 1) * SHARE)
        for share in range(SHARES):
            held[share, place, :] = rows[part, :, share * SPAN : (share + 1) * SPAN]
        outgoing.append(
            pltpu.make_async_copy(held.at[:, place, :], packed.at[:, place, :], left.at[part])
        )
        outgoing[-1].start()
    for copy in outgoing:
        copy.wait()


def pack(*sources):
    return pl.pallas_call(
        pack_kernel,
        out_shape=shape(SHARES, 4 * SHARE, SPAN),
        in_specs=[ANY] * 4,
        out_specs=ANY,
        scratch_shapes=[
            pltpu.VMEM((4, SHARE, SHARES * SPAN), BF16),
            pltpu.VMEM((SHARES, 4 * SHARE, SPAN), BF16),
            pltpu.SemaphoreType.DMA((4,)),
            pltpu.SemaphoreType.DMA((4,)),
        ],
        compiler_params=pltpu.CompilerParams(vmem_limit_bytes=60 * 1024 * 1024),
    )(*sources)


def pool_kernel(spot, whole, pooled, far_send, to_next, to_prev):
    row, token = grid(OWN, TOKENS)
    weight = jnp.zeros((OWN, TOKENS), F32)
    for level in range(LEVELS):
        shift = 4 + level
        hit = row == START[level] + lax.shift_right_logical(token, shift)
        weight = jnp.where(hit, 1.0 / (1 << shift), weight)
    weight = weight.astype(BF16)
    row, column = grid(FAR, OWN)
    valid, source = far_slot((row >> 3) ^ (spot[0] >> NEAR_BITS), row & 7)
    spread = ones(valid & (column == source))
    for part in range(2):
        rows = whole[:, part * SHARE : (part + 1) * SHARE, :].reshape(TOKENS, SPAN)
        means = dot(weight, rows, NN).astype(BF16)
        columns = slice(part * SPAN, (part + 1) * SPAN)
        pooled[:, columns] = means
        place = slice(TOKENS + part * COUNT[0], TOKENS + (part + 1) * COUNT[0])
        to_next[place, :] = means[: COUNT[0]]
        to_prev[place, :] = means[: COUNT[0]]
        far_send[:, :, columns] = dot(spread, means, NN).astype(BF16).reshape(FAR_PEERS, FAR_ROWS, SPAN)
    to_prev[:TOKENS, :] = whole[: SHARES // 2, : 2 * SHARE, :].reshape(TOKENS, SPAN)
    to_next[:TOKENS, :] = whole[SHARES // 2 :, : 2 * SHARE, :].reshape(TOKENS, SPAN)


def own_kernel(spot, pooled, own, gather, scatter, weight):
    far_at, near_at = spot[0] >> NEAR_BITS, spot[0] & (NEAR_PEERS - 1)
    index, column = grid(NEAR, OWN)
    slot, inside = near_place(index)
    valid, source = near_slot(slot ^ near_at, inside)
    own[...] = dot(ones(valid & (column == source)), pooled[...], NN)
    index, column = grid(NEAR, FAR)
    slot, inside = near_place(index)
    valid, offset, place = held_slot(inside)
    gather[...] = ones(valid & (column == (offset ^ far_at) * FAR_ROWS + place))
    row, column = grid(FAR, NEAR)
    _, inside = near_place(column)
    valid, offset, place = held_slot(inside)
    scatter[...] = ones(valid & (offset == ((row >> 3) ^ far_at)) & (place == (row & 7)))
    token, column = grid(TOKENS, FAR)
    valid, source = far_slot((column >> 3) ^ far_at, column & 7)
    result = jnp.zeros((TOKENS, FAR), F32)
    for level in range(2, LEVELS):
        shift = 4 + level
        hit = valid & (source == START[level] + (token >> shift))
        result = jnp.where(hit, 1.0 / (1 << shift), result)
    weight[...] = result.astype(BF16)


def near_kernel(own, gather, far, near_send):
    held = dot(gather[...], far[...].reshape(FAR, 2 * SPAN), NN)
    near_send[...] = (own[...] + held).astype(BF16).reshape(NEAR_PEERS, NEAR_ROWS, 2 * SPAN)


def far_send_kernel(scatter, near, far_send):
    far_send[...] = (
        dot(scatter[...], near[...].reshape(NEAR, 2 * SPAN), NN)
        .astype(BF16)
        .reshape(FAR_PEERS, FAR_ROWS, 2 * SPAN)
    )


COLUMNS = [slice(head * HEAD_DIM, (head + 1) * HEAD_DIM) for head in range(2)]
UNITS = [(head, block) for head in range(2) for block in range(2)]


def part_rows(part):
    return slice(part * SHARE, (part + 1) * SHARE)


def part_columns(part, head):
    return slice(part * SPAN + head * HEAD_DIM, part * SPAN + (head + 1) * HEAD_DIM)


def load(whole, part, block, columns):
    half = SHARES // 2
    return whole[block * half : (block + 1) * half, part_rows(part), columns].reshape(LEAF, HEAD_DIM)


def ext(whole, low, high, part, columns, store):
    half = SHARES // 2
    for place, rim in ((0, low), (LEAF + TOKENS, high)):
        store[place : place + LEAF, :] = (
            rim[:TOKENS, columns]
            .reshape(half, 2 * SHARE, HEAD_DIM)[:, part_rows(part)]
            .reshape(LEAF, HEAD_DIM)
        )
    store[LEAF : LEAF + TOKENS, :] = whole[:, part_rows(part), columns].reshape(TOKENS, HEAD_DIM)


def near_scores(spot, keys, query, block):
    window = slice(block * LEAF, block * LEAF + 3 * LEAF)
    near = dot(keys[window, :], query, NT) * (HEAD_DIM ** (-0.5) * math.log2(math.e))
    if block == 0:
        bias = jnp.where(spot[0] == 0, -1e30, 0.0).astype(F32)
        return jnp.concatenate([near[:LEAF] + bias, near[LEAF:]], axis=0)
    bias = jnp.where(spot[0] == spot[1] - 1, -1e30, 0.0).astype(F32)
    return jnp.concatenate([near[: 2 * LEAF], near[2 * LEAF :] + bias], axis=0)


def near_forward_kernel(spot, whole, low, high, mixed, stats, keys, values):
    for head, columns in enumerate(COLUMNS):
        ext(whole, low, high, 0, columns, keys.at[head])
        ext(whole, low, high, 1, columns, values.at[head])
    value_t = [jnp.transpose(values[head]) for head in range(2)]
    scores = [
        near_scores(spot, keys.at[head], load(whole, 2, block, COLUMNS[head]), block)
        for head, block in UNITS
    ]
    for unit, (head, block) in enumerate(UNITS):
        top = jnp.max(scores[unit], axis=0, keepdims=True)
        near = jnp.exp2(scores[unit] - top)
        stats[unit : unit + 1, :] = top
        stats[4 + unit : 5 + unit, :] = jnp.sum(near, axis=0, keepdims=True)
        window = slice(block * LEAF, block * LEAF + 3 * LEAF)
        mixed[unit] = dot(value_t[head][:, window], near.astype(BF16), NN)


def far_kernel(
    spot, whole, low, high, near_rows, mixed, near_stats,
    attended, far_query, stats, near_send, zero_back,
    coarse,
):
    factor = HEAD_DIM ** (-0.5)
    binary = factor * math.log2(math.e)
    even = (spot[0] & 1) == 0
    for rim, flag in ((high, even), (low, jnp.logical_not(even))):

        @pl.when(flag)
        def _():
            for part in range(2):
                summary = slice(TOKENS + part * COUNT[0], TOKENS + (part + 1) * COUNT[0])
                coarse[COARSE - COUNT[0] :, part * SPAN : (part + 1) * SPAN] = rim[summary, :]

    near_at = spot[0] & (NEAR_PEERS - 1)
    for slot in range(NEAR_PEERS):
        coarse[slot * HELD : (slot + 1) * HELD, :] = near_rows[slot, :HELD, :]
    first = NEAR_PEERS * HELD
    for offset in (2, 3):
        start = first + (offset - 2) * COUNT[1]
        coarse[start : start + COUNT[1], :] = near_rows[near_at ^ offset, HELD:, :]
    key = [coarse[:, part_columns(0, head)] for head in range(2)]
    value = [coarse[:, part_columns(1, head)] for head in range(2)]
    key_t = [jnp.transpose(key[head]) for head in range(2)]
    value_t = [jnp.transpose(value[head]) for head in range(2)]
    query = [load(whole, 2, block, COLUMNS[head]) for head, block in UNITS]
    grad = [load(whole, 3, block, COLUMNS[head]) for head, block in UNITS]
    scores = [
        dot(key[head], query[unit], NT) * binary + math.log2(RATIO)
        for unit, (head, _) in enumerate(UNITS)
    ]
    slopes = [dot(value[head], grad[unit], NT) for unit, (head, _) in enumerate(UNITS)]
    probs, lows, outs = [], [], []
    for unit, (head, block) in enumerate(UNITS):
        near_top = near_stats[unit : unit + 1, :]
        top = jnp.maximum(near_top, jnp.max(scores[unit], axis=0, keepdims=True))
        far = jnp.exp2(scores[unit] - top)
        shrink = jnp.exp2(near_top - top)
        total = near_stats[4 + unit : 5 + unit, :] * shrink + jnp.sum(far, axis=0, keepdims=True)
        inverse = 1.0 / total
        stats[unit : unit + 1, :] = top
        stats[4 + unit : 5 + unit, :] = inverse
        probs.append(far * inverse)
        lows.append(probs[unit].astype(BF16))
        outs.append(mixed[unit] * (shrink * inverse) + dot(value_t[head], lows[unit], NN))
    key_grads, value_grads = [], []
    for unit, (head, block) in enumerate(UNITS):
        grad_t = jnp.transpose(grad[unit].astype(F32))
        delta = jnp.sum(grad_t * outs[unit], axis=0, keepdims=True)
        stats[8 + unit : 9 + unit, :] = delta
        score = (probs[unit] * (slopes[unit] - delta)).astype(BF16)
        far_query[unit] = dot(key_t[head], score, NN)
        rows = slice(block * LEAF, (block + 1) * LEAF)
        attended[rows, COLUMNS[head]] = jnp.transpose(outs[unit]).astype(BF16)
        key_grads.append(dot(score, query[unit], NN))
        value_grads.append(dot(lows[unit], grad[unit], NN))
    for head in range(2):
        key_grad = ((key_grads[2 * head] + key_grads[2 * head + 1]) * factor).astype(BF16)
        value_grad = (value_grads[2 * head] + value_grads[2 * head + 1]).astype(BF16)
        for part, far_grad in ((0, key_grad), (1, value_grad)):
            place = part_columns(part, head)
            zero_back[:, place] = far_grad[first + 2 * COUNT[1] :]
            for slot in range(NEAR_PEERS):
                near_send[slot, :HELD, place] = far_grad[slot * HELD : (slot + 1) * HELD]
            for offset in (0, 1):
                near_send[near_at ^ offset, HELD:, place] = jnp.zeros((COUNT[1], HEAD_DIM), BF16)
            for offset in (2, 3):
                start = first + (offset - 2) * COUNT[1]
                near_send[near_at ^ offset, HELD:, place] = far_grad[start : start + COUNT[1]]


def backward_kernel(
    spot, whole, low, high, stats, far_query, level_zero,
    query_grad, centre, to_prev, to_next,
    keys, values,
):
    factor = HEAD_DIM ** (-0.5)
    for head, columns in enumerate(COLUMNS):
        ext(whole, low, high, 0, columns, keys.at[head])
        ext(whole, low, high, 1, columns, values.at[head])
    key_t = [jnp.transpose(keys[head]) for head in range(2)]
    query = [load(whole, 2, block, COLUMNS[head]) for head, block in UNITS]
    grad = [load(whole, 3, block, COLUMNS[head]) for head, block in UNITS]
    windows = [slice(block * LEAF, block * LEAF + 3 * LEAF) for block in range(2)]
    lows, scores = [], []
    for unit, (head, block) in enumerate(UNITS):
        near = near_scores(spot, keys.at[head], query[unit], block)
        slope = dot(values[head, windows[block], :], grad[unit], NT)
        near = jnp.exp2(near - stats[unit : unit + 1, :]) * stats[4 + unit : 5 + unit, :]
        lows.append(near.astype(BF16))
        scores.append((near * (slope - stats[8 + unit : 9 + unit, :])).astype(BF16))
    for unit, (head, block) in enumerate(UNITS):
        query_t = dot(key_t[head][:, windows[block]], scores[unit], NN) + far_query[unit]
        rows = slice(block * LEAF, (block + 1) * LEAF)
        query_grad[rows, COLUMNS[head]] = jnp.transpose(query_t * factor).astype(BF16)
    for head in range(2):
        for part, lefts, rights, scale in ((0, scores, query, factor), (1, lows, grad, None)):
            place = part_columns(part, head)
            first, second = 2 * head, 2 * head + 1
            early = dot(lefts[first], rights[first], NN)
            late = dot(lefts[second], rights[second], NN)
            if scale is not None:
                early, late = early * scale, late * scale
            to_prev[:LEAF, place] = early[:LEAF].astype(BF16)
            centre[:, place] = (early[LEAF:] + late[: 2 * LEAF]).astype(BF16)
            to_next[:LEAF, place] = late[2 * LEAF :].astype(BF16)
    to_prev[LEAF:, :] = level_zero[...]
    to_next[LEAF:, :] = level_zero[...]


def gather_kernel(
    spot, centre, from_prev, from_next, near, total, level_zero
):
    even = (spot[0] & 1) == 0
    for rim, flag in ((from_next, even), (from_prev, jnp.logical_not(even))):

        @pl.when(flag)
        def _():
            level_zero[...] = rim[LEAF:, :]

    token, column = grid(TOKENS, COUNT[0])
    own = jnp.where((token >> 4) == column, 1.0 / RATIO, 0.0).astype(BF16)
    spread = centre[...].astype(F32) + dot(own, level_zero[...], NN)
    token, column = grid(TOKENS, COUNT[1])
    own = jnp.where((token >> 5) == column, 1.0 / (2 * RATIO), 0.0).astype(BF16)
    near_at = spot[0] & (NEAR_PEERS - 1)
    for offset in (2, 3):
        spread = spread + dot(own, near[near_at ^ offset, HELD:, :], NN)
    total[:LEAF, :] = spread[:LEAF] + from_prev[:LEAF, :].astype(F32)
    total[LEAF:, :] = spread[LEAF:] + from_next[:LEAF, :].astype(F32)


def finish_kernel(total, weight, far, key_grad, value_grad):
    rows = far[...].reshape(FAR, 2 * SPAN)
    result = (total[...] + dot(weight[...], rows, NN)).astype(BF16)
    key_grad[...] = result[:, :SPAN]
    value_grad[...] = result[:, SPAN:]


FAR_GROUPS = [[far * NEAR_PEERS + near for far in range(FAR_PEERS)] for near in range(NEAR_PEERS)]
NEAR_GROUPS = [[far * NEAR_PEERS + near for near in range(NEAR_PEERS)] for far in range(FAR_PEERS)]


def body(query, key, value, cotangent):
    devices = lax.axis_size("context")
    position = lax.axis_index("context")
    spot = jnp.stack([position, jnp.int32(devices)])

    def ring(block, step):
        pairs = [(source, (source + step) % devices) for source in range(devices)]
        return lax.ppermute(block, "context", pairs)

    def exchange(block, groups):
        return lax.all_to_all(block, "context", 0, 0, axis_index_groups=groups)

    whole = lax.all_to_all(pack(key, value, query, cotangent), "head", 0, 0)
    near_slots = shape(NEAR_PEERS, NEAR_ROWS, 2 * SPAN)
    far_slots = shape(FAR_PEERS, FAR_ROWS, 2 * SPAN)
    rim = shape(TOKENS + 2 * COUNT[0], SPAN)
    pooled, far_send, to_next, to_prev = call(
        pool_kernel, (shape(OWN, 2 * SPAN), far_slots, rim, rim), specs=[SMEM, VMEM]
    )(spot, whole)
    low = ring(to_next, 1)
    high = ring(to_prev, -1)
    far = exchange(far_send, FAR_GROUPS)
    own, gather, scatter, weight = call(
        own_kernel,
        (
            shape(NEAR, 2 * SPAN, kind=F32),
            shape(NEAR, FAR),
            shape(FAR, NEAR),
            shape(TOKENS, FAR),
        ),
        specs=[SMEM, VMEM],
        cost=None,
    )(spot, pooled)
    near = exchange(call(near_kernel, near_slots, count=3)(own, gather, far), NEAR_GROUPS)
    span = 2 * LEAF + TOKENS
    sides = [pltpu.VMEM((2, span, HEAD_DIM), BF16)] * 2
    mixed, near_stats = call(
        near_forward_kernel,
        (shape(4, HEAD_DIM, LEAF, kind=F32), shape(8, LEAF, kind=F32)),
        sides,
        [SMEM] + [VMEM] * 3,
        cost=pl.CostEstimate(flops=5000000000, bytes_accessed=0, transcendentals=0),
    )(spot, whole, low, high)
    attended, far_query, stats, near_send, zero_back = call(
        far_kernel,
        (
            shape(TOKENS, SPAN),
            shape(4, HEAD_DIM, LEAF, kind=F32),
            shape(16, LEAF, kind=F32),
            near_slots,
            shape(COUNT[0], 2 * SPAN),
        ),
        [pltpu.VMEM((COARSE, 2 * SPAN), BF16)],
        [SMEM] + [VMEM] * 6,
    )(spot, whole, low, high, near, mixed, near_stats)
    near = exchange(near_send, NEAR_GROUPS)
    rim_grad = shape(LEAF + COUNT[0], 2 * SPAN)
    query_grad, centre, to_prev, to_next = call(
        backward_kernel,
        (shape(TOKENS, SPAN), shape(TOKENS, 2 * SPAN), rim_grad, rim_grad),
        sides,
        [SMEM] + [VMEM] * 6,
        cost=None,
    )(spot, whole, low, high, stats, far_query, zero_back)
    from_next = ring(to_prev, -1)
    from_prev = ring(to_next, 1)
    far = exchange(call(far_send_kernel, far_slots, count=2)(scatter, near), FAR_GROUPS)
    total = call(
        gather_kernel,
        shape(TOKENS, 2 * SPAN, kind=F32),
        [pltpu.VMEM((COUNT[0], 2 * SPAN), BF16)],
        [SMEM] + [VMEM] * 4,
        cost=pl.CostEstimate(flops=5000000000, bytes_accessed=0, transcendentals=0),
    )(spot, centre, from_prev, from_next, near)
    key_grad, value_grad = call(
        finish_kernel, (shape(TOKENS, SPAN), shape(TOKENS, SPAN)), count=3
    )(total, weight, far)
    return attended, query_grad, key_grad, value_grad


def solution(mesh):
    spec = P(("context", "head"), None)
    out = P("context", "head")
    return jax.shard_map(
        body, mesh=mesh, in_specs=(spec,) * 4, out_specs=(out,) * 4, check_vma=False
    )
```

```python
import functools
import math

import jax
import jax.numpy as jnp
from jax import lax
from jax.experimental import pallas as pl
from jax.experimental.pallas import tpu as pltpu
from jax.sharding import PartitionSpec as P

HEAD_DIM = 128
LEAF = 256
RATIO = 16
TOKENS = 512
SPAN = 256
SHARES = 8
SHARE = 64
LEVELS = 6
OWN = 64
COUNT = [32 >> level for level in range(LEVELS)]
START = [64 - (64 >> level) for level in range(LEVELS)]
FAR_PEERS = 16
FAR_ROWS = 8
FAR = FAR_PEERS * FAR_ROWS
NEAR_PEERS = 4
NEAR_BITS = 2
NEAR_ROWS = 48
HELD = 32
NEAR = NEAR_PEERS * NEAR_ROWS
COARSE = COUNT[0] + NEAR_PEERS * HELD + 2 * COUNT[1]
F32 = jnp.float32
BF16 = jnp.bfloat16
VMEM = pl.BlockSpec(memory_space=pltpu.VMEM)
SMEM = pl.BlockSpec(memory_space=pltpu.SMEM)
ANY = pl.BlockSpec(memory_space=pl.ANY)
LIMIT = pltpu.CompilerParams(vmem_limit_bytes=24 * 1024 * 1024)
NN = ((1,), (0,))
NT = ((1,), (1,))


def dot(left, right, over):
    return lax.dot_general(left, right, (over, ((), ())), preferred_element_type=F32)


def call(kernel, out_shape, scratch=(), specs=None, count=1, cost=None):
    return pl.pallas_call(
        kernel,
        out_shape=out_shape,
        in_specs=specs or [VMEM] * count,
        out_specs=jax.tree.map(lambda _: VMEM, out_shape),
        scratch_shapes=scratch,
        compiler_params=LIMIT,
        cost_estimate=cost,
    )


def shape(*sizes, kind=BF16):
    return jax.ShapeDtypeStruct(sizes, kind)


def grid(rows, columns):
    return (
        lax.broadcasted_iota(jnp.int32, (rows, columns), 0),
        lax.broadcasted_iota(jnp.int32, (rows, columns), 1),
    )


def ones(hit):
    return jnp.where(hit, 1.0, 0.0).astype(BF16)


def pick(index, cases, last):
    result = last
    for bound, value in reversed(cases):
        result = jnp.where(index < bound, value, result)
    return result


def far_slot(offset, row):
    count = pick(offset, [(1, 0), (2, COUNT[2]), (4, COUNT[3]), (8, COUNT[4])], COUNT[5])
    start = pick(offset, [(2, START[2]), (4, START[3]), (8, START[4])], START[5])
    return row < count, start + row


def near_slot(offset, row):
    return (offset >= 2) & (row >= HELD), START[1] + row - HELD


def held_slot(row):
    offset = pick(row, [(8, 1), (16, row >> 2), (24, (row >> 1) - 4)], row - 16)
    return row < HELD, offset, pick(row, [(8, row), (16, row & 3), (24, row & 1)], 0)


def near_place(index):
    slot = pick(index, [(NEAR_ROWS, 0), (2 * NEAR_ROWS, 1), (3 * NEAR_ROWS, 2)], 3)
    return slot, index - slot * NEAR_ROWS


def pack_kernel(key, value, query, cotangent, packed, rows, held, arrived, left):
    incoming = [
        pltpu.make_async_copy(source, rows.at[part], arrived.at[part])
        for part, source in enumerate((key, value, query, cotangent))
    ]
    for copy in incoming:
        copy.start()
    outgoing = []
    for part, copy in enumerate(incoming):
        copy.wait()
        place = slice(part * SHARE, (part + 1) * SHARE)
        for share in range(SHARES):
            held[share, place, :] = rows[part, :, share * SPAN : (share + 1) * SPAN]
        outgoing.append(
            pltpu.make_async_copy(held.at[:, place, :], packed.at[:, place, :], left.at[part])
        )
        outgoing[-1].start()
    for copy in outgoing:
        copy.wait()


def pack(*sources):
    return pl.pallas_call(
        pack_kernel,
        out_shape=shape(SHARES, 4 * SHARE, SPAN),
        in_specs=[ANY] * 4,
        out_specs=ANY,
        scratch_shapes=[
            pltpu.VMEM((4, SHARE, SHARES * SPAN), BF16),
            pltpu.VMEM((SHARES, 4 * SHARE, SPAN), BF16),
            pltpu.SemaphoreType.DMA((4,)),
            pltpu.SemaphoreType.DMA((4,)),
        ],
        compiler_params=pltpu.CompilerParams(vmem_limit_bytes=60 * 1024 * 1024),
    )(*sources)


def layout_kernel(spot, means, own, gather, scatter, weight):
    far_at, near_at = spot[0] >> NEAR_BITS, spot[0] & (NEAR_PEERS - 1)
    row, token = grid(FAR, TOKENS)
    valid, source = far_slot((row >> 3) ^ far_at, row & 7)
    result = jnp.zeros((FAR, TOKENS), F32)
    for level in range(2, LEVELS):
        shift = 4 + level
        hit = valid & (source == START[level] + (token >> shift))
        result = jnp.where(hit, 1.0 / (1 << shift), result)
    means[:FAR, :] = result.astype(BF16)
    row, token = grid(OWN, TOKENS)
    result = jnp.zeros((OWN, TOKENS), F32)
    for level in range(LEVELS):
        shift = 4 + level
        hit = row == START[level] + (token >> shift)
        result = jnp.where(hit, 1.0 / (1 << shift), result)
    means[FAR:, :] = result.astype(BF16)
    index, column = grid(NEAR, OWN)
    slot, inside = near_place(index)
    valid, source = near_slot(slot ^ near_at, inside)
    own[...] = ones(valid & (column == source))
    index, column = grid(NEAR, FAR)
    slot, inside = near_place(index)
    valid, offset, place = held_slot(inside)
    gather[...] = ones(valid & (column == (offset ^ far_at) * FAR_ROWS + place))
    row, column = grid(FAR, NEAR)
    _, inside = near_place(column)
    valid, offset, place = held_slot(inside)
    scatter[...] = ones(valid & (offset == ((row >> 3) ^ far_at)) & (place == (row & 7)))
    token, column = grid(TOKENS, FAR)
    valid, source = far_slot((column >> 3) ^ far_at, column & 7)
    result = jnp.zeros((TOKENS, FAR), F32)
    for level in range(2, LEVELS):
        shift = 4 + level
        hit = valid & (source == START[level] + (token >> shift))
        result = jnp.where(hit, 1.0 / (1 << shift), result)
    weight[...] = result.astype(BF16)


def pool_kernel(means, whole, pooled, far_send):
    for part in range(2):
        rows = whole[:, part_rows(part), :].reshape(TOKENS, SPAN)
        result = dot(means[...], rows, NN).astype(BF16)
        columns = slice(part * SPAN, (part + 1) * SPAN)
        far_send[:, :, columns] = result[:FAR].reshape(FAR_PEERS, FAR_ROWS, SPAN)
        pooled[:, columns] = result[FAR:]


def rim_kernel(whole, pooled, spread, to_next, to_prev, own):
    for part in range(2):
        place = slice(TOKENS + part * COUNT[0], TOKENS + (part + 1) * COUNT[0])
        means = pooled[: COUNT[0], part * SPAN : (part + 1) * SPAN]
        to_next[place, :] = means
        to_prev[place, :] = means
    to_prev[:TOKENS, :] = whole[: SHARES // 2, : 2 * SHARE, :].reshape(TOKENS, SPAN)
    to_next[:TOKENS, :] = whole[SHARES // 2 :, : 2 * SHARE, :].reshape(TOKENS, SPAN)
    own[...] = dot(spread[...], pooled[...], NN).astype(BF16)


def near_kernel(own, gather, far, near_send):
    held = dot(gather[...], far[...].reshape(FAR, 2 * SPAN), NN)
    near_send[...] = (own[...].astype(F32) + held).astype(BF16).reshape(NEAR_PEERS, NEAR_ROWS, 2 * SPAN)


def far_send_kernel(scatter, near, far_send):
    far_send[...] = (
        dot(scatter[...], near[...].reshape(NEAR, 2 * SPAN), NN)
        .astype(BF16)
        .reshape(FAR_PEERS, FAR_ROWS, 2 * SPAN)
    )


COLUMNS = [slice(head * HEAD_DIM, (head + 1) * HEAD_DIM) for head in range(2)]
UNITS = [(head, block) for head in range(2) for block in range(2)]


def part_rows(part):
    return slice(part * SHARE, (part + 1) * SHARE)


def part_columns(part, head):
    return slice(part * SPAN + head * HEAD_DIM, part * SPAN + (head + 1) * HEAD_DIM)


def load(whole, part, block, columns):
    half = SHARES // 2
    return whole[block * half : (block + 1) * half, part_rows(part), columns].reshape(LEAF, HEAD_DIM)


def ext(whole, low, high, part, columns, store):
    half = SHARES // 2
    for place, rim in ((0, low), (LEAF + TOKENS, high)):
        store[place : place + LEAF, :] = (
            rim[:TOKENS, columns]
            .reshape(half, 2 * SHARE, HEAD_DIM)[:, part_rows(part)]
            .reshape(LEAF, HEAD_DIM)
        )
    store[LEAF : LEAF + TOKENS, :] = whole[:, part_rows(part), columns].reshape(TOKENS, HEAD_DIM)


def near_scores(spot, keys, query, block):
    window = slice(block * LEAF, block * LEAF + 3 * LEAF)
    near = dot(keys[window, :], query, NT) * (HEAD_DIM ** (-0.5) * math.log2(math.e))
    if block == 0:
        bias = jnp.where(spot[0] == 0, -1e30, 0.0).astype(F32)
        return jnp.concatenate([near[:LEAF] + bias, near[LEAF:]], axis=0)
    bias = jnp.where(spot[0] == spot[1] - 1, -1e30, 0.0).astype(F32)
    return jnp.concatenate([near[: 2 * LEAF], near[2 * LEAF :] + bias], axis=0)


def near_forward_kernel(spot, whole, low, high, stats, keys):
    for head, columns in enumerate(COLUMNS):
        ext(whole, low, high, 0, columns, keys.at[head])
    scores = [
        near_scores(spot, keys.at[head], load(whole, 2, block, COLUMNS[head]), block)
        for head, block in UNITS
    ]
    for unit in range(len(UNITS)):
        top = jnp.max(scores[unit], axis=0, keepdims=True)
        near = jnp.exp2(scores[unit] - top)
        stats[unit : unit + 1, :] = top
        stats[4 + unit : 5 + unit, :] = jnp.sum(near, axis=0, keepdims=True)


def far_kernel(
    spot, whole, low, high, near_rows, near_stats,
    mixed_low, far_query, stats, near_send, zero_back,
    coarse, keys, values,
):
    factor = HEAD_DIM ** (-0.5)
    binary = factor * math.log2(math.e)
    even = (spot[0] & 1) == 0
    for rim, flag in ((high, even), (low, jnp.logical_not(even))):

        @pl.when(flag)
        def _():
            for part in range(2):
                summary = slice(TOKENS + part * COUNT[0], TOKENS + (part + 1) * COUNT[0])
                coarse[COARSE - COUNT[0] :, part * SPAN : (part + 1) * SPAN] = rim[summary, :]

    near_at = spot[0] & (NEAR_PEERS - 1)
    for slot in range(NEAR_PEERS):
        coarse[slot * HELD : (slot + 1) * HELD, :] = near_rows[slot, :HELD, :]
    first = NEAR_PEERS * HELD
    for offset in (2, 3):
        start = first + (offset - 2) * COUNT[1]
        coarse[start : start + COUNT[1], :] = near_rows[near_at ^ offset, HELD:, :]
    for head, columns in enumerate(COLUMNS):
        ext(whole, low, high, 0, columns, keys.at[head])
        ext(whole, low, high, 1, columns, values.at[head])
    near_value_t = [jnp.transpose(values[head]) for head in range(2)]
    key = [coarse[:, part_columns(0, head)] for head in range(2)]
    value = [coarse[:, part_columns(1, head)] for head in range(2)]
    key_t = [jnp.transpose(key[head]) for head in range(2)]
    value_t = [jnp.transpose(value[head]) for head in range(2)]
    query = [load(whole, 2, block, COLUMNS[head]) for head, block in UNITS]
    grad = [load(whole, 3, block, COLUMNS[head]) for head, block in UNITS]
    scores = [
        dot(key[head], query[unit], NT) * binary + math.log2(RATIO)
        for unit, (head, _) in enumerate(UNITS)
    ]
    slopes = [dot(value[head], grad[unit], NT) for unit, (head, _) in enumerate(UNITS)]
    nears = [
        near_scores(spot, keys.at[head], query[unit], block)
        for unit, (head, block) in enumerate(UNITS)
    ]
    probs, lows, outs = [], [], []
    for unit, (head, block) in enumerate(UNITS):
        near_top = near_stats[unit : unit + 1, :]
        top = jnp.maximum(near_top, jnp.max(scores[unit], axis=0, keepdims=True))
        far = jnp.exp2(scores[unit] - top)
        shrink = jnp.exp2(near_top - top)
        total = near_stats[4 + unit : 5 + unit, :] * shrink + jnp.sum(far, axis=0, keepdims=True)
        inverse = 1.0 / total
        stats[unit : unit + 1, :] = top
        stats[4 + unit : 5 + unit, :] = inverse
        probs.append(far * inverse)
        lows.append(probs[unit].astype(BF16))
        near_low = (jnp.exp2(nears[unit] - top) * inverse).astype(BF16)
        window = slice(block * LEAF, block * LEAF + 3 * LEAF)
        outs.append(
            dot(near_value_t[head][:, window], near_low, NN) + dot(value_t[head], lows[unit], NN)
        )
    key_grads, value_grads = [], []
    for unit, (head, block) in enumerate(UNITS):
        grad_t = jnp.transpose(grad[unit].astype(F32))
        delta = jnp.sum(grad_t * outs[unit], axis=0, keepdims=True)
        stats[8 + unit : 9 + unit, :] = delta
        score = (probs[unit] * (slopes[unit] - delta)).astype(BF16)
        far_query[unit] = dot(key_t[head], score, NN)
        mixed_low[unit] = outs[unit].astype(BF16)
        key_grads.append(dot(score, query[unit], NN))
        value_grads.append(dot(lows[unit], grad[unit], NN))
    for head in range(2):
        key_grad = ((key_grads[2 * head] + key_grads[2 * head + 1]) * factor).astype(BF16)
        value_grad = (value_grads[2 * head] + value_grads[2 * head + 1]).astype(BF16)
        for part, far_grad in ((0, key_grad), (1, value_grad)):
            place = part_columns(part, head)
            zero_back[:, place] = far_grad[first + 2 * COUNT[1] :]
            for slot in range(NEAR_PEERS):
                near_send[slot, :HELD, place] = far_grad[slot * HELD : (slot + 1) * HELD]
            for offset in (0, 1):
                near_send[near_at ^ offset, HELD:, place] = jnp.zeros((COUNT[1], HEAD_DIM), BF16)
            for offset in (2, 3):
                start = first + (offset - 2) * COUNT[1]
                near_send[near_at ^ offset, HELD:, place] = far_grad[start : start + COUNT[1]]


def rim_grad_kernel(block, spot, whole, rim, stats, level_zero, other, target, attended=None):
    factor = HEAD_DIM ** (-0.5)
    edge = 0 if block == 0 else spot[1] - 1
    bias = jnp.where(spot[0] == edge, -1e30, 0.0).astype(F32)
    half = SHARES // 2
    keys, values = [
        [
            rim[:TOKENS, COLUMNS[head]]
            .reshape(half, 2 * SHARE, HEAD_DIM)[:, part_rows(part)]
            .reshape(LEAF, HEAD_DIM)
            for head in range(2)
        ]
        for part in range(2)
    ]
    query = [load(whole, 2, block, COLUMNS[head]) for head in range(2)]
    grad = [load(whole, 3, block, COLUMNS[head]) for head in range(2)]
    near = [dot(keys[head], query[head], NT) for head in range(2)]
    slope = [dot(values[head], grad[head], NT) for head in range(2)]
    lows, scores = [], []
    for head in range(2):
        unit = 2 * head + block
        probs = near[head] * (factor * math.log2(math.e)) + bias
        probs = jnp.exp2(probs - stats[unit : unit + 1, :]) * stats[4 + unit : 5 + unit, :]
        lows.append(probs.astype(BF16))
        scores.append((probs * (slope[head] - stats[8 + unit : 9 + unit, :])).astype(BF16))
    for head in range(2):
        target[:LEAF, part_columns(0, head)] = (dot(scores[head], query[head], NN) * factor).astype(BF16)
        target[:LEAF, part_columns(1, head)] = dot(lows[head], grad[head], NN).astype(BF16)
    target[LEAF:, :] = level_zero[...]
    if attended is not None:
        for unit, (head, block) in enumerate(UNITS):
            rows = slice(block * LEAF, (block + 1) * LEAF)
            attended[rows, COLUMNS[head]] = jnp.transpose(other[unit])


def backward_kernel(
    spot, whole, low, high, stats, far_query,
    query_grad, centre,
    keys, values,
):
    factor = HEAD_DIM ** (-0.5)
    for head, columns in enumerate(COLUMNS):
        ext(whole, low, high, 0, columns, keys.at[head])
        ext(whole, low, high, 1, columns, values.at[head])
    key_t = [jnp.transpose(keys[head]) for head in range(2)]
    query = [load(whole, 2, block, COLUMNS[head]) for head, block in UNITS]
    grad = [load(whole, 3, block, COLUMNS[head]) for head, block in UNITS]
    windows = [slice(block * LEAF, block * LEAF + 3 * LEAF) for block in range(2)]
    lows, scores = [], []
    for unit, (head, block) in enumerate(UNITS):
        near = near_scores(spot, keys.at[head], query[unit], block)
        slope = dot(values[head, windows[block], :], grad[unit], NT)
        near = jnp.exp2(near - stats[unit : unit + 1, :]) * stats[4 + unit : 5 + unit, :]
        lows.append(near.astype(BF16))
        scores.append((near * (slope - stats[8 + unit : 9 + unit, :])).astype(BF16))
    for unit, (head, block) in enumerate(UNITS):
        query_t = dot(key_t[head][:, windows[block]], scores[unit], NN) + far_query[unit]
        rows = slice(block * LEAF, (block + 1) * LEAF)
        query_grad[rows, COLUMNS[head]] = jnp.transpose(query_t * factor).astype(BF16)
    for head in range(2):
        for part, lefts, rights, scale in ((0, scores, query, factor), (1, lows, grad, None)):
            place = part_columns(part, head)
            first, second = 2 * head, 2 * head + 1
            early = dot(lefts[first][LEAF:], rights[first], NN)
            late = dot(lefts[second][: 2 * LEAF], rights[second], NN)
            if scale is not None:
                early, late = early * scale, late * scale
            centre[:, place] = (early + late).astype(BF16)


def gather_kernel(spot, centre, from_prev, near, total, zero_weight):
    token, column = grid(TOKENS, COUNT[0])
    odd = jnp.where((spot[0] & 1) == 1, 1.0 / RATIO, 0.0).astype(F32)
    even = 1.0 / RATIO - odd
    own = (token >> 4) == column
    zero_weight[...] = jnp.where(own, even, 0.0).astype(BF16)
    spread = dot(jnp.where(own, odd, 0.0).astype(BF16), from_prev[LEAF:, :], NN)
    spread = spread + centre[...].astype(F32)
    token, column = grid(TOKENS, COUNT[1])
    own = jnp.where((token >> 5) == column, 1.0 / (2 * RATIO), 0.0).astype(BF16)
    near_at = spot[0] & (NEAR_PEERS - 1)
    for offset in (2, 3):
        spread = spread + dot(own, near[near_at ^ offset, HELD:, :], NN)
    total[:LEAF, :] = spread[:LEAF] + from_prev[:LEAF, :].astype(F32)
    total[LEAF:, :] = spread[LEAF:]


def finish_kernel(total, weight, zero_weight, far, from_next, key_grad, value_grad):
    rows = far[...].reshape(FAR, 2 * SPAN)
    result = total[...] + dot(weight[...], rows, NN) + dot(zero_weight[...], from_next[LEAF:, :], NN)
    low = result[:LEAF].astype(BF16)
    high = (result[LEAF:] + from_next[:LEAF, :].astype(F32)).astype(BF16)
    for block, part in ((0, low), (1, high)):
        rows = slice(block * LEAF, (block + 1) * LEAF)
        key_grad[rows, :] = part[:, :SPAN]
        value_grad[rows, :] = part[:, SPAN:]


FAR_GROUPS = [[far * NEAR_PEERS + near for far in range(FAR_PEERS)] for near in range(NEAR_PEERS)]
NEAR_GROUPS = [[far * NEAR_PEERS + near for near in range(NEAR_PEERS)] for far in range(FAR_PEERS)]


def body(query, key, value, cotangent):
    devices = lax.axis_size("context")
    position = lax.axis_index("context")
    spot = jnp.stack([position, jnp.int32(devices)])

    def ring(block, step):
        pairs = [(source, (source + step) % devices) for source in range(devices)]
        return lax.ppermute(block, "context", pairs)

    def exchange(block, groups):
        return lax.all_to_all(block, "context", 0, 0, axis_index_groups=groups)

    whole = lax.all_to_all(pack(key, value, query, cotangent), "head", 0, 0)
    near_slots = shape(NEAR_PEERS, NEAR_ROWS, 2 * SPAN)
    far_slots = shape(FAR_PEERS, FAR_ROWS, 2 * SPAN)
    rim = shape(TOKENS + 2 * COUNT[0], SPAN)
    means, spread, gather, scatter, weight = call(
        layout_kernel,
        (
            shape(FAR + OWN, TOKENS),
            shape(NEAR, OWN),
            shape(NEAR, FAR),
            shape(FAR, NEAR),
            shape(TOKENS, FAR),
        ),
        specs=[SMEM],
        cost=None,
    )(spot)
    pooled, far_send = call(pool_kernel, (shape(OWN, 2 * SPAN), far_slots), count=2)(means, whole)
    to_next, to_prev, own = call(rim_kernel, (rim, rim, shape(NEAR, 2 * SPAN)), count=3)(
        whole, pooled, spread
    )
    low = ring(to_next, 1)
    high = ring(to_prev, -1)
    far = exchange(far_send, FAR_GROUPS)
    near = exchange(call(near_kernel, near_slots, count=3)(own, gather, far), NEAR_GROUPS)
    span = 2 * LEAF + TOKENS
    sides = [pltpu.VMEM((2, span, HEAD_DIM), BF16)] * 2
    near_stats = call(
        near_forward_kernel,
        shape(8, LEAF, kind=F32),
        sides[:1],
        [SMEM] + [VMEM] * 3,
        cost=pl.CostEstimate(flops=5000000000, bytes_accessed=0, transcendentals=0),
    )(spot, whole, low, high)
    mixed_low, far_query, stats, near_send, zero_back = call(
        far_kernel,
        (
            shape(4, HEAD_DIM, LEAF),
            shape(4, HEAD_DIM, LEAF, kind=F32),
            shape(16, LEAF, kind=F32),
            near_slots,
            shape(COUNT[0], 2 * SPAN),
        ),
        [pltpu.VMEM((COARSE, 2 * SPAN), BF16)] + sides,
        [SMEM] + [VMEM] * 5,
    )(spot, whole, low, high, near, near_stats)
    near = exchange(near_send, NEAR_GROUPS)
    rim_grad = shape(LEAF + COUNT[0], 2 * SPAN)
    to_next, attended = call(
        functools.partial(rim_grad_kernel, 1),
        (rim_grad, shape(TOKENS, SPAN)),
        specs=[SMEM] + [VMEM] * 5,
        cost=pl.CostEstimate(flops=5000000000, bytes_accessed=0, transcendentals=0),
    )(spot, whole, high, stats, zero_back, mixed_low)
    from_prev = ring(to_next, 1)
    far = exchange(call(far_send_kernel, far_slots, count=2)(scatter, near), FAR_GROUPS)
    to_prev = call(
        functools.partial(rim_grad_kernel, 0), rim_grad, specs=[SMEM] + [VMEM] * 5, cost=None
    )(spot, whole, low, stats, zero_back, from_prev)
    from_next = ring(to_prev, -1)
    query_grad, centre = call(
        backward_kernel,
        (shape(TOKENS, SPAN), shape(TOKENS, 2 * SPAN)),
        sides,
        [SMEM] + [VMEM] * 5,
        cost=pl.CostEstimate(flops=5000000000, bytes_accessed=0, transcendentals=0),
    )(spot, whole, low, high, stats, far_query)
    total, zero_weight = call(
        gather_kernel,
        (shape(TOKENS, 2 * SPAN, kind=F32), shape(TOKENS, COUNT[0])),
        specs=[SMEM] + [VMEM] * 3,
        cost=None,
    )(spot, centre, from_prev, near)
    key_grad, value_grad = call(
        finish_kernel, (shape(TOKENS, SPAN), shape(TOKENS, SPAN)), count=5
    )(total, weight, zero_weight, far, from_next)
    return attended, query_grad, key_grad, value_grad


def solution(mesh):
    spec = P(("context", "head"), None)
    out = P("context", "head")
    return jax.shard_map(
        body, mesh=mesh, in_specs=(spec,) * 4, out_specs=(out,) * 4, check_vma=False
    )
```

```python
import functools
import math

import jax
import jax.numpy as jnp
from jax import lax
from jax.experimental import pallas as pl
from jax.experimental.pallas import tpu as pltpu
from jax.sharding import PartitionSpec as P

HEAD_DIM = 128
LEAF = 256
RATIO = 16
TOKENS = 512
SPAN = 256
SHARES = 8
SHARE = 64
LEVELS = 6
OWN = 64
COUNT = [32 >> level for level in range(LEVELS)]
START = [64 - (64 >> level) for level in range(LEVELS)]
FAR_PEERS = 16
FAR_ROWS = 8
FAR = FAR_PEERS * FAR_ROWS
NEAR_PEERS = 4
NEAR_BITS = 2
NEAR_ROWS = 48
HELD = 32
NEAR = NEAR_PEERS * NEAR_ROWS
COARSE = COUNT[0] + NEAR_PEERS * HELD + 2 * COUNT[1]
F32 = jnp.float32
BF16 = jnp.bfloat16
VMEM = pl.BlockSpec(memory_space=pltpu.VMEM)
SMEM = pl.BlockSpec(memory_space=pltpu.SMEM)
ANY = pl.BlockSpec(memory_space=pl.ANY)
LIMIT = pltpu.CompilerParams(vmem_limit_bytes=24 * 1024 * 1024)
NN = ((1,), (0,))
NT = ((1,), (1,))


def dot(left, right, over):
    return lax.dot_general(left, right, (over, ((), ())), preferred_element_type=F32)


def call(kernel, out_shape, scratch=(), specs=None, count=1, cost=None):
    return pl.pallas_call(
        kernel,
        out_shape=out_shape,
        in_specs=specs or [VMEM] * count,
        out_specs=jax.tree.map(lambda _: VMEM, out_shape),
        scratch_shapes=scratch,
        compiler_params=LIMIT,
        cost_estimate=cost,
    )


def shape(*sizes, kind=BF16):
    return jax.ShapeDtypeStruct(sizes, kind)


def grid(rows, columns):
    return (
        lax.broadcasted_iota(jnp.int32, (rows, columns), 0),
        lax.broadcasted_iota(jnp.int32, (rows, columns), 1),
    )


def ones(hit):
    return jnp.where(hit, 1.0, 0.0).astype(BF16)


def pick(index, cases, last):
    result = last
    for bound, value in reversed(cases):
        result = jnp.where(index < bound, value, result)
    return result


def far_slot(offset, row):
    count = pick(offset, [(1, 0), (2, COUNT[2]), (4, COUNT[3]), (8, COUNT[4])], COUNT[5])
    start = pick(offset, [(2, START[2]), (4, START[3]), (8, START[4])], START[5])
    return row < count, start + row


def near_slot(offset, row):
    return (offset >= 2) & (row >= HELD), START[1] + row - HELD


def held_slot(row):
    offset = pick(row, [(8, 1), (16, row >> 2), (24, (row >> 1) - 4)], row - 16)
    return row < HELD, offset, pick(row, [(8, row), (16, row & 3), (24, row & 1)], 0)


def near_place(index):
    slot = pick(index, [(NEAR_ROWS, 0), (2 * NEAR_ROWS, 1), (3 * NEAR_ROWS, 2)], 3)
    return slot, index - slot * NEAR_ROWS


def pack_kernel(key, value, query, cotangent, packed, rows, held, arrived, left):
    incoming = [
        pltpu.make_async_copy(source, rows.at[part], arrived.at[part])
        for part, source in enumerate((key, value, query, cotangent))
    ]
    for copy in incoming:
        copy.start()
    outgoing = []
    for part, copy in enumerate(incoming):
        copy.wait()
        place = slice(part * SHARE, (part + 1) * SHARE)
        for share in range(SHARES):
            held[share, place, :] = rows[part, :, share * SPAN : (share + 1) * SPAN]
        outgoing.append(
            pltpu.make_async_copy(held.at[:, place, :], packed.at[:, place, :], left.at[part])
        )
        outgoing[-1].start()
    for copy in outgoing:
        copy.wait()


def pack(*sources):
    return pl.pallas_call(
        pack_kernel,
        out_shape=shape(SHARES, 4 * SHARE, SPAN),
        in_specs=[ANY] * 4,
        out_specs=ANY,
        scratch_shapes=[
            pltpu.VMEM((4, SHARE, SHARES * SPAN), BF16),
            pltpu.VMEM((SHARES, 4 * SHARE, SPAN), BF16),
            pltpu.SemaphoreType.DMA((4,)),
            pltpu.SemaphoreType.DMA((4,)),
        ],
        compiler_params=pltpu.CompilerParams(vmem_limit_bytes=60 * 1024 * 1024),
    )(*sources)


def layout_kernel(spot, means, own, gather, scatter, weight):
    far_at, near_at = spot[0] >> NEAR_BITS, spot[0] & (NEAR_PEERS - 1)
    row, token = grid(FAR, TOKENS)
    valid, source = far_slot((row >> 3) ^ far_at, row & 7)
    result = jnp.zeros((FAR, TOKENS), F32)
    for level in range(2, LEVELS):
        shift = 4 + level
        hit = valid & (source == START[level] + (token >> shift))
        result = jnp.where(hit, 1.0 / (1 << shift), result)
    means[:FAR, :] = result.astype(BF16)
    row, token = grid(OWN, TOKENS)
    result = jnp.zeros((OWN, TOKENS), F32)
    for level in range(LEVELS):
        shift = 4 + level
        hit = row == START[level] + (token >> shift)
        result = jnp.where(hit, 1.0 / (1 << shift), result)
    means[FAR:, :] = result.astype(BF16)
    index, column = grid(NEAR, OWN)
    slot, inside = near_place(index)
    valid, source = near_slot(slot ^ near_at, inside)
    own[...] = ones(valid & (column == source))
    index, column = grid(NEAR, FAR)
    slot, inside = near_place(index)
    valid, offset, place = held_slot(inside)
    gather[...] = ones(valid & (column == (offset ^ far_at) * FAR_ROWS + place))
    row, column = grid(FAR, NEAR)
    _, inside = near_place(column)
    valid, offset, place = held_slot(inside)
    scatter[...] = ones(valid & (offset == ((row >> 3) ^ far_at)) & (place == (row & 7)))
    token, column = grid(TOKENS, FAR)
    valid, source = far_slot((column >> 3) ^ far_at, column & 7)
    result = jnp.zeros((TOKENS, FAR), F32)
    for level in range(2, LEVELS):
        shift = 4 + level
        hit = valid & (source == START[level] + (token >> shift))
        result = jnp.where(hit, 1.0 / (1 << shift), result)
    weight[...] = result.astype(BF16)


def pool_kernel(means, whole, pooled, far_send):
    for part in range(2):
        rows = whole[:, part_rows(part), :].reshape(TOKENS, SPAN)
        result = dot(means[...], rows, NN).astype(BF16)
        columns = slice(part * SPAN, (part + 1) * SPAN)
        far_send[:, :, columns] = result[:FAR].reshape(FAR_PEERS, FAR_ROWS, SPAN)
        pooled[:, columns] = result[FAR:]


def rim_kernel(spot, whole, pooled, spread, to_pair, to_other, own):
    half = SHARES // 2
    upper = (1 - (spot[0] & 1)) * half
    to_pair[:TOKENS, :] = whole[pl.ds(upper, half), : 2 * SHARE, :].reshape(TOKENS, SPAN)
    to_other[...] = whole[pl.ds(half - upper, half), : 2 * SHARE, :].reshape(TOKENS, SPAN)
    for part in range(2):
        place = slice(TOKENS + part * COUNT[0], TOKENS + (part + 1) * COUNT[0])
        to_pair[place, :] = pooled[: COUNT[0], part * SPAN : (part + 1) * SPAN]
    own[...] = dot(spread[...], pooled[...], NN).astype(BF16)


def near_kernel(own, gather, far, near_send):
    held = dot(gather[...], far[...].reshape(FAR, 2 * SPAN), NN)
    near_send[...] = (own[...].astype(F32) + held).astype(BF16).reshape(NEAR_PEERS, NEAR_ROWS, 2 * SPAN)


def far_send_kernel(scatter, near, far_send):
    far_send[...] = (
        dot(scatter[...], near[...].reshape(NEAR, 2 * SPAN), NN)
        .astype(BF16)
        .reshape(FAR_PEERS, FAR_ROWS, 2 * SPAN)
    )


COLUMNS = [slice(head * HEAD_DIM, (head + 1) * HEAD_DIM) for head in range(2)]
UNITS = [(head, block) for head in range(2) for block in range(2)]


def part_rows(part):
    return slice(part * SHARE, (part + 1) * SHARE)


def part_columns(part, head):
    return slice(part * SPAN + head * HEAD_DIM, part * SPAN + (head + 1) * HEAD_DIM)


def load(whole, part, block, columns):
    half = SHARES // 2
    return whole[block * half : (block + 1) * half, part_rows(part), columns].reshape(LEAF, HEAD_DIM)


def rim_rows(rim, part, columns):
    half = SHARES // 2
    return (
        rim[:TOKENS, columns]
        .reshape(half, 2 * SHARE, HEAD_DIM)[:, part_rows(part)]
        .reshape(LEAF, HEAD_DIM)
    )


def ext(spot, whole, pair, other, part, columns, store):
    odd = spot[0] & 1
    far_end = LEAF + TOKENS
    place = pl.multiple_of((1 - odd) * far_end, LEAF)
    store[pl.ds(place, LEAF), :] = rim_rows(pair, part, columns)
    place = pl.multiple_of(odd * far_end, LEAF)
    store[pl.ds(place, LEAF), :] = rim_rows(other, part, columns)
    store[LEAF : LEAF + TOKENS, :] = whole[:, part_rows(part), columns].reshape(TOKENS, HEAD_DIM)


def near_scores(spot, keys, query, block):
    window = slice(block * LEAF, block * LEAF + 3 * LEAF)
    near = dot(keys[window, :], query, NT) * (HEAD_DIM ** (-0.5) * math.log2(math.e))
    if block == 0:
        bias = jnp.where(spot[0] == 0, -1e30, 0.0).astype(F32)
        return jnp.concatenate([near[:LEAF] + bias, near[LEAF:]], axis=0)
    bias = jnp.where(spot[0] == spot[1] - 1, -1e30, 0.0).astype(F32)
    return jnp.concatenate([near[: 2 * LEAF], near[2 * LEAF :] + bias], axis=0)


def near_forward_kernel(spot, whole, pair, other, stats, keys):
    for head, columns in enumerate(COLUMNS):
        ext(spot, whole, pair, other, 0, columns, keys.at[head])
    scores = [
        near_scores(spot, keys.at[head], load(whole, 2, block, COLUMNS[head]), block)
        for head, block in UNITS
    ]
    for unit in range(len(UNITS)):
        top = jnp.max(scores[unit], axis=0, keepdims=True)
        near = jnp.exp2(scores[unit] - top)
        stats[unit : unit + 1, :] = top
        stats[4 + unit : 5 + unit, :] = jnp.sum(near, axis=0, keepdims=True)


def far_kernel(
    spot, whole, pair, other, near_rows, near_stats,
    mixed_low, far_query, stats, near_send, zero_back,
    coarse, keys, values,
):
    factor = HEAD_DIM ** (-0.5)
    binary = factor * math.log2(math.e)
    for part in range(2):
        summary = slice(TOKENS + part * COUNT[0], TOKENS + (part + 1) * COUNT[0])
        coarse[COARSE - COUNT[0] :, part * SPAN : (part + 1) * SPAN] = pair[summary, :]
    near_at = spot[0] & (NEAR_PEERS - 1)
    for slot in range(NEAR_PEERS):
        coarse[slot * HELD : (slot + 1) * HELD, :] = near_rows[slot, :HELD, :]
    first = NEAR_PEERS * HELD
    for offset in (2, 3):
        start = first + (offset - 2) * COUNT[1]
        coarse[start : start + COUNT[1], :] = near_rows[near_at ^ offset, HELD:, :]
    for head, columns in enumerate(COLUMNS):
        ext(spot, whole, pair, other, 0, columns, keys.at[head])
        ext(spot, whole, pair, other, 1, columns, values.at[head])
    near_value_t = [jnp.transpose(values[head]) for head in range(2)]
    key = [coarse[:, part_columns(0, head)] for head in range(2)]
    value = [coarse[:, part_columns(1, head)] for head in range(2)]
    key_t = [jnp.transpose(key[head]) for head in range(2)]
    value_t = [jnp.transpose(value[head]) for head in range(2)]
    query = [load(whole, 2, block, COLUMNS[head]) for head, block in UNITS]
    grad = [load(whole, 3, block, COLUMNS[head]) for head, block in UNITS]
    scores = [
        dot(key[head], query[unit], NT) * binary + math.log2(RATIO)
        for unit, (head, _) in enumerate(UNITS)
    ]
    slopes = [dot(value[head], grad[unit], NT) for unit, (head, _) in enumerate(UNITS)]
    nears = [
        near_scores(spot, keys.at[head], query[unit], block)
        for unit, (head, block) in enumerate(UNITS)
    ]
    probs, lows, outs = [], [], []
    for unit, (head, block) in enumerate(UNITS):
        near_top = near_stats[unit : unit + 1, :]
        top = jnp.maximum(near_top, jnp.max(scores[unit], axis=0, keepdims=True))
        far = jnp.exp2(scores[unit] - top)
        shrink = jnp.exp2(near_top - top)
        total = near_stats[4 + unit : 5 + unit, :] * shrink + jnp.sum(far, axis=0, keepdims=True)
        inverse = 1.0 / total
        stats[unit : unit + 1, :] = top
        stats[4 + unit : 5 + unit, :] = inverse
        probs.append(far * inverse)
        lows.append(probs[unit].astype(BF16))
        near_low = (jnp.exp2(nears[unit] - top) * inverse).astype(BF16)
        window = slice(block * LEAF, block * LEAF + 3 * LEAF)
        outs.append(
            dot(near_value_t[head][:, window], near_low, NN) + dot(value_t[head], lows[unit], NN)
        )
    key_grads, value_grads = [], []
    for unit, (head, block) in enumerate(UNITS):
        grad_t = jnp.transpose(grad[unit].astype(F32))
        delta = jnp.sum(grad_t * outs[unit], axis=0, keepdims=True)
        stats[8 + unit : 9 + unit, :] = delta
        score = (probs[unit] * (slopes[unit] - delta)).astype(BF16)
        far_query[unit] = dot(key_t[head], score, NN)
        mixed_low[unit] = outs[unit].astype(BF16)
        key_grads.append(dot(score, query[unit], NN))
        value_grads.append(dot(lows[unit], grad[unit], NN))
    for head in range(2):
        key_grad = ((key_grads[2 * head] + key_grads[2 * head + 1]) * factor).astype(BF16)
        value_grad = (value_grads[2 * head] + value_grads[2 * head + 1]).astype(BF16)
        for part, far_grad in ((0, key_grad), (1, value_grad)):
            place = part_columns(part, head)
            zero_back[:, place] = far_grad[first + 2 * COUNT[1] :]
            for slot in range(NEAR_PEERS):
                near_send[slot, :HELD, place] = far_grad[slot * HELD : (slot + 1) * HELD]
            for offset in (0, 1):
                near_send[near_at ^ offset, HELD:, place] = jnp.zeros((COUNT[1], HEAD_DIM), BF16)
            for offset in (2, 3):
                start = first + (offset - 2) * COUNT[1]
                near_send[near_at ^ offset, HELD:, place] = far_grad[start : start + COUNT[1]]


def rim_grads(spot, whole, rim, stats, block, bias):
    factor = HEAD_DIM ** (-0.5)
    half = SHARES // 2
    rows = pl.ds(block * half, half)
    query, grad = [
        [
            whole[rows, part_rows(part), COLUMNS[head]].reshape(LEAF, HEAD_DIM)
            for head in range(2)
        ]
        for part in (2, 3)
    ]
    near = [dot(rim_rows(rim, 0, COLUMNS[head]), query[head], NT) for head in range(2)]
    slope = [dot(rim_rows(rim, 1, COLUMNS[head]), grad[head], NT) for head in range(2)]
    lows, scores = [], []
    for head in range(2):
        unit = 2 * head + block
        probs = near[head] * (factor * math.log2(math.e)) + bias
        probs = jnp.exp2(probs - stats[pl.ds(unit, 1), :]) * stats[pl.ds(4 + unit, 1), :]
        lows.append(probs.astype(BF16))
        scores.append((probs * (slope[head] - stats[pl.ds(8 + unit, 1), :])).astype(BF16))
    return [
        (
            part_columns(part, head),
            ((dot(scores[head], query[head], NN) * factor) if part == 0 else dot(lows[head], grad[head], NN)).astype(BF16),
        )
        for head in range(2)
        for part in range(2)
    ]


def pair_grad_kernel(spot, whole, pair, stats, level_zero, mixed_low, to_pair, attended):
    for place, result in rim_grads(spot, whole, pair, stats, 1 - (spot[0] & 1), 0.0):
        to_pair[:LEAF, place] = result
    to_pair[LEAF:, :] = level_zero[...]
    for unit, (head, block) in enumerate(UNITS):
        rows = slice(block * LEAF, (block + 1) * LEAF)
        attended[rows, COLUMNS[head]] = jnp.transpose(mixed_low[unit])


def other_grad_kernel(spot, whole, other, stats, _after, to_other):
    edge = (spot[0] == 0) | (spot[0] == spot[1] - 1)
    bias = jnp.where(edge, -1e30, 0.0).astype(F32)
    for place, result in rim_grads(spot, whole, other, stats, spot[0] & 1, bias):
        to_other[:, place] = result


def backward_kernel(
    spot, whole, pair, other, stats, far_query,
    query_grad, centre,
    keys, values,
):
    factor = HEAD_DIM ** (-0.5)
    for head, columns in enumerate(COLUMNS):
        ext(spot, whole, pair, other, 0, columns, keys.at[head])
        ext(spot, whole, pair, other, 1, columns, values.at[head])
    key_t = [jnp.transpose(keys[head]) for head in range(2)]
    query = [load(whole, 2, block, COLUMNS[head]) for head, block in UNITS]
    grad = [load(whole, 3, block, COLUMNS[head]) for head, block in UNITS]
    windows = [slice(block * LEAF, block * LEAF + 3 * LEAF) for block in range(2)]
    lows, scores = [], []
    for unit, (head, block) in enumerate(UNITS):
        near = near_scores(spot, keys.at[head], query[unit], block)
        slope = dot(values[head, windows[block], :], grad[unit], NT)
        near = jnp.exp2(near - stats[unit : unit + 1, :]) * stats[4 + unit : 5 + unit, :]
        lows.append(near.astype(BF16))
        scores.append((near * (slope - stats[8 + unit : 9 + unit, :])).astype(BF16))
    for unit, (head, block) in enumerate(UNITS):
        query_t = dot(key_t[head][:, windows[block]], scores[unit], NN) + far_query[unit]
        rows = slice(block * LEAF, (block + 1) * LEAF)
        query_grad[rows, COLUMNS[head]] = jnp.transpose(query_t * factor).astype(BF16)
    for head in range(2):
        for part, lefts, rights, scale in ((0, scores, query, factor), (1, lows, grad, None)):
            place = part_columns(part, head)
            first, second = 2 * head, 2 * head + 1
            early = dot(lefts[first][LEAF:], rights[first], NN)
            late = dot(lefts[second][: 2 * LEAF], rights[second], NN)
            if scale is not None:
                early, late = early * scale, late * scale
            centre[:, place] = (early + late).astype(BF16)


def gather_kernel(spot, centre, from_pair, near, total):
    token, column = grid(TOKENS, COUNT[0])
    own = jnp.where((token >> 4) == column, 1.0 / RATIO, 0.0).astype(BF16)
    spread = centre[...].astype(F32) + dot(own, from_pair[LEAF:, :], NN)
    token, column = grid(TOKENS, COUNT[1])
    own = jnp.where((token >> 5) == column, 1.0 / (2 * RATIO), 0.0).astype(BF16)
    near_at = spot[0] & (NEAR_PEERS - 1)
    for offset in (2, 3):
        spread = spread + dot(own, near[near_at ^ offset, HELD:, :], NN)
    total[...] = spread
    rows = pl.ds(pl.multiple_of((1 - (spot[0] & 1)) * LEAF, LEAF), LEAF)
    total[rows, :] += from_pair[:LEAF, :].astype(F32)


def finish_kernel(spot, total, weight, far, from_other, key_grad, value_grad):
    rows = far[...].reshape(FAR, 2 * SPAN)
    odd = spot[0] & 1
    near = pl.ds(pl.multiple_of(odd * LEAF, LEAF), LEAF)
    rest = pl.ds(pl.multiple_of((1 - odd) * LEAF, LEAF), LEAF)
    first = total[near, :] + dot(weight[near, :], rows, NN) + from_other[...].astype(F32)
    second = total[rest, :] + dot(weight[rest, :], rows, NN)
    for place, result in ((near, first.astype(BF16)), (rest, second.astype(BF16))):
        key_grad[place, :] = result[:, :SPAN]
        value_grad[place, :] = result[:, SPAN:]


FAR_GROUPS = [[far * NEAR_PEERS + near for far in range(FAR_PEERS)] for near in range(NEAR_PEERS)]
NEAR_GROUPS = [[far * NEAR_PEERS + near for near in range(NEAR_PEERS)] for far in range(FAR_PEERS)]


def body(query, key, value, cotangent):
    devices = lax.axis_size("context")
    position = lax.axis_index("context")
    spot = jnp.stack([position, jnp.int32(devices)])

    def swap(block, odd_step):
        pairs = [
            (source, (source + (odd_step if source % 2 else -odd_step)) % devices)
            for source in range(devices)
        ]
        return lax.ppermute(block, "context", pairs)

    def exchange(block, groups):
        return lax.all_to_all(block, "context", 0, 0, axis_index_groups=groups)

    whole = lax.all_to_all(pack(key, value, query, cotangent), "head", 0, 0)
    near_slots = shape(NEAR_PEERS, NEAR_ROWS, 2 * SPAN)
    far_slots = shape(FAR_PEERS, FAR_ROWS, 2 * SPAN)
    rim = shape(TOKENS + 2 * COUNT[0], SPAN)
    means, spread, gather, scatter, weight = call(
        layout_kernel,
        (
            shape(FAR + OWN, TOKENS),
            shape(NEAR, OWN),
            shape(NEAR, FAR),
            shape(FAR, NEAR),
            shape(TOKENS, FAR),
        ),
        specs=[SMEM],
        cost=None,
    )(spot)
    pooled, far_send = call(pool_kernel, (shape(OWN, 2 * SPAN), far_slots), count=2)(means, whole)
    to_pair, to_other, own = call(
        rim_kernel,
        (rim, shape(TOKENS, SPAN), shape(NEAR, 2 * SPAN)),
        specs=[SMEM] + [VMEM] * 3,
    )(spot, whole, pooled, spread)
    pair = swap(to_pair, -1)
    other = swap(to_other, 1)
    far = exchange(far_send, FAR_GROUPS)
    near = exchange(call(near_kernel, near_slots, count=3)(own, gather, far), NEAR_GROUPS)
    span = 2 * LEAF + TOKENS
    sides = [pltpu.VMEM((2, span, HEAD_DIM), BF16)] * 2
    near_stats = call(
        near_forward_kernel,
        shape(8, LEAF, kind=F32),
        sides[:1],
        [SMEM] + [VMEM] * 3,
        cost=pl.CostEstimate(flops=5000000000, bytes_accessed=0, transcendentals=0),
    )(spot, whole, pair, other)
    mixed_low, far_query, stats, near_send, zero_back = call(
        far_kernel,
        (
            shape(4, HEAD_DIM, LEAF),
            shape(4, HEAD_DIM, LEAF, kind=F32),
            shape(16, LEAF, kind=F32),
            near_slots,
            shape(COUNT[0], 2 * SPAN),
        ),
        [pltpu.VMEM((COARSE, 2 * SPAN), BF16)] + sides,
        [SMEM] + [VMEM] * 5,
    )(spot, whole, pair, other, near, near_stats)
    near = exchange(near_send, NEAR_GROUPS)
    rim_grad = shape(LEAF + COUNT[0], 2 * SPAN)
    to_pair, attended = call(
        pair_grad_kernel,
        (rim_grad, shape(TOKENS, SPAN)),
        specs=[SMEM] + [VMEM] * 5,
        cost=pl.CostEstimate(flops=5000000000, bytes_accessed=0, transcendentals=0),
    )(spot, whole, pair, stats, zero_back, mixed_low)
    from_pair = swap(to_pair, -1)
    far = exchange(call(far_send_kernel, far_slots, count=2)(scatter, near), FAR_GROUPS)
    to_other = call(
        other_grad_kernel, shape(LEAF, 2 * SPAN), specs=[SMEM] + [VMEM] * 4, cost=None
    )(spot, whole, other, stats, from_pair)
    from_other = swap(to_other, 1)
    query_grad, centre = call(
        backward_kernel,
        (shape(TOKENS, SPAN), shape(TOKENS, 2 * SPAN)),
        sides,
        [SMEM] + [VMEM] * 5,
        cost=pl.CostEstimate(flops=5000000000, bytes_accessed=0, transcendentals=0),
    )(spot, whole, pair, other, stats, far_query)
    total = call(
        gather_kernel, shape(TOKENS, 2 * SPAN, kind=F32), specs=[SMEM] + [VMEM] * 3, cost=None
    )(spot, centre, from_pair, near)
    key_grad, value_grad = call(
        finish_kernel, (shape(TOKENS, SPAN), shape(TOKENS, SPAN)), specs=[SMEM] + [VMEM] * 4
    )(spot, total, weight, far, from_other)
    return attended, query_grad, key_grad, value_grad


def solution(mesh):
    spec = P(("context", "head"), None)
    out = P("context", "head")
    return jax.shard_map(
        body, mesh=mesh, in_specs=(spec,) * 4, out_specs=(out,) * 4, check_vma=False
    )
```

```python
import functools
import math

import jax
import jax.numpy as jnp
from jax import lax
from jax.experimental import pallas as pl
from jax.experimental.pallas import tpu as pltpu
from jax.sharding import PartitionSpec as P

HEAD_DIM = 128
LEAF = 256
RATIO = 16
TOKENS = 512
SPAN = 256
SHARES = 8
SHARE = 64
LEVELS = 6
OWN = 64
COUNT = [32 >> level for level in range(LEVELS)]
START = [64 - (64 >> level) for level in range(LEVELS)]
FAR_PEERS = 16
FAR_ROWS = 8
FAR = FAR_PEERS * FAR_ROWS
NEAR_PEERS = 4
NEAR_BITS = 2
NEAR_ROWS = 48
HELD = 32
NEAR = NEAR_PEERS * NEAR_ROWS
COARSE = COUNT[0] + NEAR_PEERS * HELD + 2 * COUNT[1]
F32 = jnp.float32
BF16 = jnp.bfloat16
VMEM = pl.BlockSpec(memory_space=pltpu.VMEM)
SMEM = pl.BlockSpec(memory_space=pltpu.SMEM)
ANY = pl.BlockSpec(memory_space=pl.ANY)
LIMIT = pltpu.CompilerParams(vmem_limit_bytes=24 * 1024 * 1024)
NN = ((1,), (0,))
NT = ((1,), (1,))


def dot(left, right, over):
    return lax.dot_general(left, right, (over, ((), ())), preferred_element_type=F32)


def call(kernel, out_shape, scratch=(), specs=None, count=1, cost=None):
    return pl.pallas_call(
        kernel,
        out_shape=out_shape,
        in_specs=specs or [VMEM] * count,
        out_specs=jax.tree.map(lambda _: VMEM, out_shape),
        scratch_shapes=scratch,
        compiler_params=LIMIT,
        cost_estimate=cost,
    )


def shape(*sizes, kind=BF16):
    return jax.ShapeDtypeStruct(sizes, kind)


def grid(rows, columns):
    return (
        lax.broadcasted_iota(jnp.int32, (rows, columns), 0),
        lax.broadcasted_iota(jnp.int32, (rows, columns), 1),
    )


def ones(hit):
    return jnp.where(hit, 1.0, 0.0).astype(BF16)


def pick(index, cases, last):
    result = last
    for bound, value in reversed(cases):
        result = jnp.where(index < bound, value, result)
    return result


def far_slot(offset, row):
    count = pick(offset, [(1, 0), (2, COUNT[2]), (4, COUNT[3]), (8, COUNT[4])], COUNT[5])
    start = pick(offset, [(2, START[2]), (4, START[3]), (8, START[4])], START[5])
    return row < count, start + row


def near_slot(offset, row):
    return (offset >= 2) & (row >= HELD), START[1] + row - HELD


def held_slot(row):
    offset = pick(row, [(8, 1), (16, row >> 2), (24, (row >> 1) - 4)], row - 16)
    return row < HELD, offset, pick(row, [(8, row), (16, row & 3), (24, row & 1)], 0)


def near_place(index):
    slot = pick(index, [(NEAR_ROWS, 0), (2 * NEAR_ROWS, 1), (3 * NEAR_ROWS, 2)], 3)
    return slot, index - slot * NEAR_ROWS


def pack_kernel(key, value, query, cotangent, packed, rows, held, arrived, left):
    incoming = [
        pltpu.make_async_copy(source, rows.at[part], arrived.at[part])
        for part, source in enumerate((key, value, query, cotangent))
    ]
    for copy in incoming:
        copy.start()
    outgoing = []
    for part, copy in enumerate(incoming):
        copy.wait()
        place = slice(part * SHARE, (part + 1) * SHARE)
        for share in range(SHARES):
            held[share, place, :] = rows[part, :, share * SPAN : (share + 1) * SPAN]
        outgoing.append(
            pltpu.make_async_copy(held.at[:, place, :], packed.at[:, place, :], left.at[part])
        )
        outgoing[-1].start()
    for copy in outgoing:
        copy.wait()


def pack(*sources):
    return pl.pallas_call(
        pack_kernel,
        out_shape=shape(SHARES, 4 * SHARE, SPAN),
        in_specs=[ANY] * 4,
        out_specs=ANY,
        scratch_shapes=[
            pltpu.VMEM((4, SHARE, SHARES * SPAN), BF16),
            pltpu.VMEM((SHARES, 4 * SHARE, SPAN), BF16),
            pltpu.SemaphoreType.DMA((4,)),
            pltpu.SemaphoreType.DMA((4,)),
        ],
        compiler_params=pltpu.CompilerParams(vmem_limit_bytes=60 * 1024 * 1024),
    )(*sources)


def layout_kernel(spot, means, own, gather, scatter, weight):
    far_at, near_at = spot[0] >> NEAR_BITS, spot[0] & (NEAR_PEERS - 1)
    row, token = grid(FAR, TOKENS)
    valid, source = far_slot((row >> 3) ^ far_at, row & 7)
    result = jnp.zeros((FAR, TOKENS), F32)
    for level in range(2, LEVELS):
        shift = 4 + level
        hit = valid & (source == START[level] + (token >> shift))
        result = jnp.where(hit, 1.0 / (1 << shift), result)
    means[:FAR, :] = result.astype(BF16)
    row, token = grid(OWN, TOKENS)
    result = jnp.zeros((OWN, TOKENS), F32)
    for level in range(LEVELS):
        shift = 4 + level
        hit = row == START[level] + (token >> shift)
        result = jnp.where(hit, 1.0 / (1 << shift), result)
    means[FAR:, :] = result.astype(BF16)
    index, column = grid(NEAR, OWN)
    slot, inside = near_place(index)
    valid, source = near_slot(slot ^ near_at, inside)
    own[...] = ones(valid & (column == source))
    index, column = grid(NEAR, FAR)
    slot, inside = near_place(index)
    valid, offset, place = held_slot(inside)
    gather[...] = ones(valid & (column == (offset ^ far_at) * FAR_ROWS + place))
    row, column = grid(FAR, NEAR)
    _, inside = near_place(column)
    valid, offset, place = held_slot(inside)
    scatter[...] = ones(valid & (offset == ((row >> 3) ^ far_at)) & (place == (row & 7)))
    token, column = grid(TOKENS, FAR)
    valid, source = far_slot((column >> 3) ^ far_at, column & 7)
    result = jnp.zeros((TOKENS, FAR), F32)
    for level in range(2, LEVELS):
        shift = 4 + level
        hit = valid & (source == START[level] + (token >> shift))
        result = jnp.where(hit, 1.0 / (1 << shift), result)
    weight[...] = result.astype(BF16)


def pool_kernel(means, whole, pooled, far_send):
    for part in range(2):
        rows = whole[:, part_rows(part), :].reshape(TOKENS, SPAN)
        result = dot(means[...], rows, NN).astype(BF16)
        columns = slice(part * SPAN, (part + 1) * SPAN)
        far_send[:, :, columns] = result[:FAR].reshape(FAR_PEERS, FAR_ROWS, SPAN)
        pooled[:, columns] = result[FAR:]


def rim_kernel(whole, pooled, spread, to_next, to_prev, own):
    for part in range(2):
        place = slice(TOKENS + part * COUNT[0], TOKENS + (part + 1) * COUNT[0])
        means = pooled[: COUNT[0], part * SPAN : (part + 1) * SPAN]
        to_next[place, :] = means
        to_prev[place, :] = means
    to_prev[:TOKENS, :] = whole[: SHARES // 2, : 2 * SHARE, :].reshape(TOKENS, SPAN)
    to_next[:TOKENS, :] = whole[SHARES // 2 :, : 2 * SHARE, :].reshape(TOKENS, SPAN)
    own[...] = dot(spread[...], pooled[...], NN).astype(BF16)


def near_kernel(own, gather, far, near_send):
    held = dot(gather[...], far[...].reshape(FAR, 2 * SPAN), NN)
    near_send[...] = (own[...].astype(F32) + held).astype(BF16).reshape(NEAR_PEERS, NEAR_ROWS, 2 * SPAN)


def far_send_kernel(scatter, near, far_send):
    far_send[...] = (
        dot(scatter[...], near[...].reshape(NEAR, 2 * SPAN), NN)
        .astype(BF16)
        .reshape(FAR_PEERS, FAR_ROWS, 2 * SPAN)
    )


COLUMNS = [slice(head * HEAD_DIM, (head + 1) * HEAD_DIM) for head in range(2)]
UNITS = [(head, block) for head in range(2) for block in range(2)]


def part_rows(part):
    return slice(part * SHARE, (part + 1) * SHARE)


def part_columns(part, head):
    return slice(part * SPAN + head * HEAD_DIM, part * SPAN + (head + 1) * HEAD_DIM)


def load(whole, part, block, columns):
    half = SHARES // 2
    return whole[block * half : (block + 1) * half, part_rows(part), columns].reshape(LEAF, HEAD_DIM)


def ext(whole, low, high, part, columns, store):
    half = SHARES // 2
    for place, rim in ((0, low), (LEAF + TOKENS, high)):
        store[place : place + LEAF, :] = (
            rim[:TOKENS, columns]
            .reshape(half, 2 * SHARE, HEAD_DIM)[:, part_rows(part)]
            .reshape(LEAF, HEAD_DIM)
        )
    store[LEAF : LEAF + TOKENS, :] = whole[:, part_rows(part), columns].reshape(TOKENS, HEAD_DIM)


def near_scores(spot, keys, query, block):
    window = slice(block * LEAF, block * LEAF + 3 * LEAF)
    near = dot(keys[window, :], query, NT) * (HEAD_DIM ** (-0.5) * math.log2(math.e))
    if block == 0:
        bias = jnp.where(spot[0] == 0, -1e30, 0.0).astype(F32)
        return jnp.concatenate([near[:LEAF] + bias, near[LEAF:]], axis=0)
    bias = jnp.where(spot[0] == spot[1] - 1, -1e30, 0.0).astype(F32)
    return jnp.concatenate([near[: 2 * LEAF], near[2 * LEAF :] + bias], axis=0)


def near_forward_kernel(spot, whole, low, high, stats, keys):
    for head, columns in enumerate(COLUMNS):
        ext(whole, low, high, 0, columns, keys.at[head])
    scores = [
        near_scores(spot, keys.at[head], load(whole, 2, block, COLUMNS[head]), block)
        for head, block in UNITS
    ]
    for unit in range(len(UNITS)):
        top = jnp.max(scores[unit], axis=0, keepdims=True)
        near = jnp.exp2(scores[unit] - top)
        stats[unit : unit + 1, :] = top
        stats[4 + unit : 5 + unit, :] = jnp.sum(near, axis=0, keepdims=True)


def far_kernel(
    spot, whole, low, high, near_rows, near_stats,
    mixed_low, far_query, stats, near_send, zero_back,
    coarse, keys, values,
):
    factor = HEAD_DIM ** (-0.5)
    binary = factor * math.log2(math.e)
    even = (spot[0] & 1) == 0
    for rim, flag in ((high, even), (low, jnp.logical_not(even))):

        @pl.when(flag)
        def _():
            for part in range(2):
                summary = slice(TOKENS + part * COUNT[0], TOKENS + (part + 1) * COUNT[0])
                coarse[COARSE - COUNT[0] :, part * SPAN : (part + 1) * SPAN] = rim[summary, :]

    near_at = spot[0] & (NEAR_PEERS - 1)
    for slot in range(NEAR_PEERS):
        coarse[slot * HELD : (slot + 1) * HELD, :] = near_rows[slot, :HELD, :]
    first = NEAR_PEERS * HELD
    for offset in (2, 3):
        start = first + (offset - 2) * COUNT[1]
        coarse[start : start + COUNT[1], :] = near_rows[near_at ^ offset, HELD:, :]
    for head, columns in enumerate(COLUMNS):
        ext(whole, low, high, 0, columns, keys.at[head])
        ext(whole, low, high, 1, columns, values.at[head])
    near_value_t = [jnp.transpose(values[head]) for head in range(2)]
    key = [coarse[:, part_columns(0, head)] for head in range(2)]
    value = [coarse[:, part_columns(1, head)] for head in range(2)]
    key_t = [jnp.transpose(key[head]) for head in range(2)]
    value_t = [jnp.transpose(value[head]) for head in range(2)]
    query = [load(whole, 2, block, COLUMNS[head]) for head, block in UNITS]
    grad = [load(whole, 3, block, COLUMNS[head]) for head, block in UNITS]
    scores = [
        dot(key[head], query[unit], NT) * binary + math.log2(RATIO)
        for unit, (head, _) in enumerate(UNITS)
    ]
    slopes = [dot(value[head], grad[unit], NT) for unit, (head, _) in enumerate(UNITS)]
    nears = [
        near_scores(spot, keys.at[head], query[unit], block)
        for unit, (head, block) in enumerate(UNITS)
    ]
    probs, lows, outs = [], [], []
    for unit, (head, block) in enumerate(UNITS):
        near_top = near_stats[unit : unit + 1, :]
        top = jnp.maximum(near_top, jnp.max(scores[unit], axis=0, keepdims=True))
        far = jnp.exp2(scores[unit] - top)
        shrink = jnp.exp2(near_top - top)
        total = near_stats[4 + unit : 5 + unit, :] * shrink + jnp.sum(far, axis=0, keepdims=True)
        inverse = 1.0 / total
        stats[unit : unit + 1, :] = top
        stats[4 + unit : 5 + unit, :] = inverse
        probs.append(far * inverse)
        lows.append(probs[unit].astype(BF16))
        near_low = (jnp.exp2(nears[unit] - top) * inverse).astype(BF16)
        window = slice(block * LEAF, block * LEAF + 3 * LEAF)
        outs.append(
            dot(near_value_t[head][:, window], near_low, NN) + dot(value_t[head], lows[unit], NN)
        )
    key_grads, value_grads = [], []
    for unit, (head, block) in enumerate(UNITS):
        grad_t = jnp.transpose(grad[unit].astype(F32))
        delta = jnp.sum(grad_t * outs[unit], axis=0, keepdims=True)
        stats[8 + unit : 9 + unit, :] = delta
        score = (probs[unit] * (slopes[unit] - delta)).astype(BF16)
        far_query[unit] = dot(key_t[head], score, NN)
        mixed_low[unit] = outs[unit].astype(BF16)
        key_grads.append(dot(score, query[unit], NN))
        value_grads.append(dot(lows[unit], grad[unit], NN))
    for head in range(2):
        key_grad = ((key_grads[2 * head] + key_grads[2 * head + 1]) * factor).astype(BF16)
        value_grad = (value_grads[2 * head] + value_grads[2 * head + 1]).astype(BF16)
        for part, far_grad in ((0, key_grad), (1, value_grad)):
            place = part_columns(part, head)
            zero_back[:, place] = far_grad[first + 2 * COUNT[1] :]
            for slot in range(NEAR_PEERS):
                near_send[slot, :HELD, place] = far_grad[slot * HELD : (slot + 1) * HELD]
            for offset in (0, 1):
                near_send[near_at ^ offset, HELD:, place] = jnp.zeros((COUNT[1], HEAD_DIM), BF16)
            for offset in (2, 3):
                start = first + (offset - 2) * COUNT[1]
                near_send[near_at ^ offset, HELD:, place] = far_grad[start : start + COUNT[1]]


def rim_grad_kernel(block, spot, whole, rim, stats, level_zero, other, target, attended=None):
    factor = HEAD_DIM ** (-0.5)
    edge = 0 if block == 0 else spot[1] - 1
    bias = jnp.where(spot[0] == edge, -1e30, 0.0).astype(F32)
    half = SHARES // 2
    keys, values = [
        [
            rim[:TOKENS, COLUMNS[head]]
            .reshape(half, 2 * SHARE, HEAD_DIM)[:, part_rows(part)]
            .reshape(LEAF, HEAD_DIM)
            for head in range(2)
        ]
        for part in range(2)
    ]
    query = [load(whole, 2, block, COLUMNS[head]) for head in range(2)]
    grad = [load(whole, 3, block, COLUMNS[head]) for head in range(2)]
    near = [dot(keys[head], query[head], NT) for head in range(2)]
    slope = [dot(values[head], grad[head], NT) for head in range(2)]
    lows, scores = [], []
    for head in range(2):
        unit = 2 * head + block
        probs = near[head] * (factor * math.log2(math.e)) + bias
        probs = jnp.exp2(probs - stats[unit : unit + 1, :]) * stats[4 + unit : 5 + unit, :]
        lows.append(probs.astype(BF16))
        scores.append((probs * (slope[head] - stats[8 + unit : 9 + unit, :])).astype(BF16))
    for head in range(2):
        target[:LEAF, part_columns(0, head)] = (dot(scores[head], query[head], NN) * factor).astype(BF16)
        target[:LEAF, part_columns(1, head)] = dot(lows[head], grad[head], NN).astype(BF16)
    target[LEAF:, :] = level_zero[...]
    if attended is not None:
        for unit, (head, block) in enumerate(UNITS):
            rows = slice(block * LEAF, (block + 1) * LEAF)
            attended[rows, COLUMNS[head]] = jnp.transpose(other[unit])


def backward_kernel(
    spot, whole, low, high, stats, far_query,
    query_grad, centre,
    keys, values,
):
    factor = HEAD_DIM ** (-0.5)
    for head, columns in enumerate(COLUMNS):
        ext(whole, low, high, 0, columns, keys.at[head])
        ext(whole, low, high, 1, columns, values.at[head])
    key_t = [jnp.transpose(keys[head]) for head in range(2)]
    query = [load(whole, 2, block, COLUMNS[head]) for head, block in UNITS]
    grad = [load(whole, 3, block, COLUMNS[head]) for head, block in UNITS]
    windows = [slice(block * LEAF, block * LEAF + 3 * LEAF) for block in range(2)]
    lows, scores = [], []
    for unit, (head, block) in enumerate(UNITS):
        near = near_scores(spot, keys.at[head], query[unit], block)
        slope = dot(values[head, windows[block], :], grad[unit], NT)
        near = jnp.exp2(near - stats[unit : unit + 1, :]) * stats[4 + unit : 5 + unit, :]
        lows.append(near.astype(BF16))
        scores.append((near * (slope - stats[8 + unit : 9 + unit, :])).astype(BF16))
    for unit, (head, block) in enumerate(UNITS):
        query_t = dot(key_t[head][:, windows[block]], scores[unit], NN) + far_query[unit]
        rows = slice(block * LEAF, (block + 1) * LEAF)
        query_grad[rows, COLUMNS[head]] = jnp.transpose(query_t * factor).astype(BF16)
    for head in range(2):
        for part, lefts, rights, scale in ((0, scores, query, factor), (1, lows, grad, None)):
            place = part_columns(part, head)
            first, second = 2 * head, 2 * head + 1
            early = dot(lefts[first][LEAF:], rights[first], NN)
            late = dot(lefts[second][: 2 * LEAF], rights[second], NN)
            if scale is not None:
                early, late = early * scale, late * scale
            centre[:, place] = (early + late).astype(BF16)


def gather_kernel(spot, centre, from_next, near, total, zero_weight):
    token, column = grid(TOKENS, COUNT[0])
    odd = jnp.where((spot[0] & 1) == 1, 1.0 / RATIO, 0.0).astype(F32)
    even = 1.0 / RATIO - odd
    own = (token >> 4) == column
    zero_weight[...] = jnp.where(own, odd, 0.0).astype(BF16)
    spread = dot(jnp.where(own, even, 0.0).astype(BF16), from_next[LEAF:, :], NN)
    spread = spread + centre[...].astype(F32)
    token, column = grid(TOKENS, COUNT[1])
    own = jnp.where((token >> 5) == column, 1.0 / (2 * RATIO), 0.0).astype(BF16)
    near_at = spot[0] & (NEAR_PEERS - 1)
    for offset in (2, 3):
        spread = spread + dot(own, near[near_at ^ offset, HELD:, :], NN)
    total[:LEAF, :] = spread[:LEAF]
    total[LEAF:, :] = spread[LEAF:] + from_next[:LEAF, :].astype(F32)


def finish_kernel(total, weight, zero_weight, far, from_prev, key_grad, value_grad):
    rows = far[...].reshape(FAR, 2 * SPAN)
    result = total[...] + dot(weight[...], rows, NN) + dot(zero_weight[...], from_prev[LEAF:, :], NN)
    low = (result[:LEAF] + from_prev[:LEAF, :].astype(F32)).astype(BF16)
    high = result[LEAF:].astype(BF16)
    for block, part in ((0, low), (1, high)):
        rows = slice(block * LEAF, (block + 1) * LEAF)
        key_grad[rows, :] = part[:, :SPAN]
        value_grad[rows, :] = part[:, SPAN:]


FAR_GROUPS = [[far * NEAR_PEERS + near for far in range(FAR_PEERS)] for near in range(NEAR_PEERS)]
NEAR_GROUPS = [[far * NEAR_PEERS + near for near in range(NEAR_PEERS)] for far in range(FAR_PEERS)]


def body(query, key, value, cotangent):
    devices = lax.axis_size("context")
    position = lax.axis_index("context")
    spot = jnp.stack([position, jnp.int32(devices)])

    def ring(block, step):
        pairs = [(source, (source + step) % devices) for source in range(devices)]
        return lax.ppermute(block, "context", pairs)

    def exchange(block, groups):
        return lax.all_to_all(block, "context", 0, 0, axis_index_groups=groups)

    whole = lax.all_to_all(pack(key, value, query, cotangent), "head", 0, 0)
    near_slots = shape(NEAR_PEERS, NEAR_ROWS, 2 * SPAN)
    far_slots = shape(FAR_PEERS, FAR_ROWS, 2 * SPAN)
    rim = shape(TOKENS + 2 * COUNT[0], SPAN)
    means, spread, gather, scatter, weight = call(
        layout_kernel,
        (
            shape(FAR + OWN, TOKENS),
            shape(NEAR, OWN),
            shape(NEAR, FAR),
            shape(FAR, NEAR),
            shape(TOKENS, FAR),
        ),
        specs=[SMEM],
        cost=None,
    )(spot)
    pooled, far_send = call(pool_kernel, (shape(OWN, 2 * SPAN), far_slots), count=2)(means, whole)
    to_next, to_prev, own = call(rim_kernel, (rim, rim, shape(NEAR, 2 * SPAN)), count=3)(
        whole, pooled, spread
    )
    low = ring(to_next, 1)
    high = ring(to_prev, -1)
    far = exchange(far_send, FAR_GROUPS)
    near = exchange(call(near_kernel, near_slots, count=3)(own, gather, far), NEAR_GROUPS)
    span = 2 * LEAF + TOKENS
    sides = [pltpu.VMEM((2, span, HEAD_DIM), BF16)] * 2
    near_stats = call(
        near_forward_kernel,
        shape(8, LEAF, kind=F32),
        sides[:1],
        [SMEM] + [VMEM] * 3,
        cost=pl.CostEstimate(flops=5000000000, bytes_accessed=0, transcendentals=0),
    )(spot, whole, low, high)
    mixed_low, far_query, stats, near_send, zero_back = call(
        far_kernel,
        (
            shape(4, HEAD_DIM, LEAF),
            shape(4, HEAD_DIM, LEAF, kind=F32),
            shape(16, LEAF, kind=F32),
            near_slots,
            shape(COUNT[0], 2 * SPAN),
        ),
        [pltpu.VMEM((COARSE, 2 * SPAN), BF16)] + sides,
        [SMEM] + [VMEM] * 5,
    )(spot, whole, low, high, near, near_stats)
    near = exchange(near_send, NEAR_GROUPS)
    rim_grad = shape(LEAF + COUNT[0], 2 * SPAN)
    to_prev, attended = call(
        functools.partial(rim_grad_kernel, 0),
        (rim_grad, shape(TOKENS, SPAN)),
        specs=[SMEM] + [VMEM] * 5,
        cost=pl.CostEstimate(flops=5000000000, bytes_accessed=0, transcendentals=0),
    )(spot, whole, low, stats, zero_back, mixed_low)
    from_next = ring(to_prev, -1)
    far = exchange(call(far_send_kernel, far_slots, count=2)(scatter, near), FAR_GROUPS)
    to_next = call(
        functools.partial(rim_grad_kernel, 1), rim_grad, specs=[SMEM] + [VMEM] * 5, cost=None
    )(spot, whole, high, stats, zero_back, from_next)
    from_prev = ring(to_next, 1)
    query_grad, centre = call(
        backward_kernel,
        (shape(TOKENS, SPAN), shape(TOKENS, 2 * SPAN)),
        sides,
        [SMEM] + [VMEM] * 5,
        cost=pl.CostEstimate(flops=5000000000, bytes_accessed=0, transcendentals=0),
    )(spot, whole, low, high, stats, far_query)
    total, zero_weight = call(
        gather_kernel,
        (shape(TOKENS, 2 * SPAN, kind=F32), shape(TOKENS, COUNT[0])),
        specs=[SMEM] + [VMEM] * 3,
        cost=None,
    )(spot, centre, from_next, near)
    key_grad, value_grad = call(
        finish_kernel, (shape(TOKENS, SPAN), shape(TOKENS, SPAN)), count=5
    )(total, weight, zero_weight, far, from_prev)
    return attended, query_grad, key_grad, value_grad


def solution(mesh):
    spec = P(("context", "head"), None)
    out = P("context", "head")
    return jax.shard_map(
        body, mesh=mesh, in_specs=(spec,) * 4, out_specs=(out,) * 4, check_vma=False
    )
```
